512 devices in a mesh: pipe: 16 (over z_lo, y), expert: 32 (over z_hi, x, core).
Axes of the slice: x: 4, y: 4, z: 16 (z_hi: 4, z_lo: 4; z = z_hi * 4 + z_lo), core: 2. Of those that a mesh axis runs over, the one named last changes fastest.
Arguments:
- act_prev: bfloat16 [16, 2048, 4096], P('pipe', 'expert'), may hold values from -6 to 6
- fwd_routes: int32 [16, 2048, 1], P('pipe', 'expert'), may hold values from 0 to 3; in each aligned block of 64 rows (0 to 63, 64 to 127, ..., all dimensions but the last counted through in order) at most 24 rows name the same one
- fwd_gates: float32 [16, 2048, 1], P('pipe', 'expert'), may hold values from 0.25 to 1.5
- saved_input: bfloat16 [16, 2048, 4096], P('pipe', 'expert'), may hold values from -6 to 6
- grad_prev: bfloat16 [16, 2048, 4096], P('pipe', 'expert'), may hold values from -6 to 6
- bwd_routes: int32 [16, 2048, 1], P('pipe', 'expert'), may hold values from 0 to 3; in each aligned block of 64 rows (0 to 63, 64 to 127, ..., all dimensions but the last counted through in order) at most 24 rows name the same one
- bwd_gates: float32 [16, 2048, 1], P('pipe', 'expert'), may hold values from 0.25 to 1.5
- norm_gain: float32 [16, 4096], P('pipe'), may hold values from 0.1 to 1.9
- w_up: bfloat16 [16, 32, 1024, 512], P('pipe', 'expert'), may hold values from -0.09375 to 0.09375
- w_down: bfloat16 [16, 32, 1024, 512], P('pipe', 'expert'), may hold values from -0.1875 to 0.1875
Outputs:
- section_out: bfloat16 [16, 2048, 4096], P('pipe', 'expert')
- input_grad: bfloat16 [16, 2048, 4096], P('pipe', 'expert')
The draws below stay inside these ranges and needn't reach their ends.
Inputs may be any that keep to these rules, and one draw needn't show every extreme that they name: `fwd_routes`: the 1 ids of a token differ; among the 64 rows of one device (aligned blocks) no id is named by more than 24 rows, a bound that some block reaches. `bwd_routes`: the 1 ids of a token differ; among the 64 rows of one device (aligned blocks) no id is named by more than 24 rows, a bound that some block reaches.
All inputs are finite; a program needn't handle non-finite values.
Results may differ from the reference program's by a relative error of at most 0.0054.
Values may be sent and summed in bfloat16 or wider, within the bound.
A program may use at most 64 MiB of HBM per device.

```python
import math
import jax
import jax.numpy as jnp
import numpy as np
from jax import lax

D = 4096
HE = 1024
TOPK = 1
TOK = 64
HSPLIT = 8
EXPERTS = 4
CAP = 24
TOKENS = 2048
N_PIPE = 16
N_EXPERT = 32


def levels(own_key, shape, pieces, low, top_value):
    loudness, own = 1.0, jax.random.fold_in(own_key, 6)
    for position, parts in pieces:
        draws = jnp.exp(jax.random.uniform(jax.random.fold_in(own, position), (parts,), jnp.float32, low / len(pieces), top_value / len(pieces)))
        loudness = loudness * jnp.repeat(draws, shape[position] // parts).reshape([-1 if axis == position else 1 for axis in range(len(shape))])
    return loudness


def deal_out(stream_key, own, number, rows, number_of, top, bound, skew):
    ranking = jax.random.permutation(stream_key, number_of)
    heavy_load, common = portions_of(number_of, rows * top, bound, skew, True), portions_of(number_of, rows * top, bound, skew, False)
    places = jnp.arange(number_of)

    def named(sizes, turn):
        used = int((sizes > 0).sum())
        fixed = max(1, used // 4)
        shifted = fixed + (places - fixed + turn * (used - fixed)) % max(1, number_of - fixed)
        return jnp.zeros((number_of,), jnp.int32).at[ranking[jnp.where(places < fixed, places, shifted)]].set(jnp.asarray(sizes, jnp.int32))

    sizes = jnp.where(number % 4 == 0, named(heavy_load, number // 4), named(common, number - number // 4 - 1))
    mixed = jax.random.permutation(jax.random.fold_in(own, 3), number_of)
    giver, receiver = mixed[0:number_of // 2 * 2:2], mixed[1:number_of // 2 * 2:2]
    room = jnp.minimum(sizes[giver] - 1, bound - sizes[receiver]) // 2
    room = jnp.where((giver == ranking[0]) | (receiver == ranking[0]) | (sizes[receiver] == 0), 0, jnp.maximum(room, 0))
    shifted = jax.random.randint(jax.random.fold_in(own, 4), (number_of // 2,), 0, 1 << 20) % (room + 1)
    sizes = sizes.at[giver].add(-shifted).at[receiver].add(shifted)
    labels = jnp.searchsorted(jnp.cumsum(sizes), jnp.arange(rows * top), side="right").astype(jnp.int32)
    listing = labels.reshape(top, rows).T
    listing = listing[jax.random.permutation(jax.random.fold_in(own, 1), rows)]
    turn = jax.random.randint(jax.random.fold_in(own, 2), (rows, 1), 0, top)
    return jnp.take_along_axis(listing, (jnp.arange(top)[None, :] + turn) % top, axis=1)


def portions_of(amount, total, reach, lean, full):
    portions = [(1 << 20) // math.isqrt(rank ** lean) + 1 for rank in range(1, amount + 1)]
    largest = reach if full else min(reach, max(-(-total // amount), total * portions[0] // sum(portions)))
    least = 1 if total - largest >= amount - 1 else 0
    counts, rest = [largest] + [least] * (amount - 1), total - largest - least * (amount - 1)
    while rest > 0:
        candidates = [i for i in range(1, amount) if counts[i] < largest] or [i for i in range(1, amount) if counts[i] < reach]
        whole, budget = sum([portions[i] for i in candidates]), rest
        for i in candidates:
            more = min(reach - counts[i], max(1, budget * portions[i] // whole), rest)
            counts[i] = counts[i] + more
            rest = rest - more
    return np.array(counts)


def bell_draw(stream_key, shape, spread, reach, shards=(), held_as=jnp.bfloat16):
    loudness = levels(stream_key, shape, shards, -0.22, 0.18) if shards else 1.0
    entries = jax.random.normal(stream_key, shape, jnp.float32) * spread * loudness
    return jnp.minimum(jnp.maximum(entries, -reach), reach).astype(held_as)


def setup_inputs(seed: int = 0) -> dict:
    streams_of = jax.random.split(jax.random.key(seed), 11)
    act_prev = bell_draw(streams_of[0], (N_PIPE, TOKENS, D), 1.0, 6.0, ((0, 16), (1, 32)))
    fwd_routes_keys = jax.random.split(jax.random.fold_in(streams_of[1], 1), N_PIPE * TOKENS // TOK)
    fwd_routes_turns = jax.random.permutation(jax.random.fold_in(streams_of[1], 3), N_PIPE * TOKENS // TOK)
    fwd_routes = jax.vmap(lambda own, number: deal_out(jax.random.fold_in(streams_of[1], 2), own, number, TOK, EXPERTS, TOPK, CAP, 2))(fwd_routes_keys, fwd_routes_turns).reshape((N_PIPE, TOKENS, TOPK))
    fwd_gates = jnp.clip(0.25 + 1.25 * jax.random.uniform(streams_of[2], (N_PIPE, TOKENS, TOPK), jnp.float32) ** levels(streams_of[2], (N_PIPE, TOKENS, TOPK), ((0, 16), (1, 32)), -0.2, 0.2), 0.25, 1.5)
    saved_input = bell_draw(streams_of[3], (N_PIPE, TOKENS, D), 1.0, 6.0, ((0, 16), (1, 32)))
    grad_prev = bell_draw(streams_of[4], (N_PIPE, TOKENS, D), 1.0, 6.0, ((0, 16), (1, 32)))
    bwd_routes_keys = jax.random.split(jax.random.fold_in(streams_of[5], 1), N_PIPE * TOKENS // TOK)
    bwd_routes_turns = jax.random.permutation(jax.random.fold_in(streams_of[5], 3), N_PIPE * TOKENS // TOK)
    bwd_routes = jax.vmap(lambda own, number: deal_out(jax.random.fold_in(streams_of[5], 2), own, number, TOK, EXPERTS, TOPK, CAP, 2))(bwd_routes_keys, bwd_routes_turns).reshape((N_PIPE, TOKENS, TOPK))
    bwd_gates = jnp.clip(0.25 + 1.25 * jax.random.uniform(streams_of[6], (N_PIPE, TOKENS, TOPK), jnp.float32) ** levels(streams_of[6], (N_PIPE, TOKENS, TOPK), ((0, 16), (1, 32)), -0.2, 0.2), 0.25, 1.5)
    norm_gain = jnp.clip(1.0 + 0.18 * jax.random.normal(streams_of[7], (N_PIPE, D), jnp.float32), 0.1, 1.9)
    w_up = bell_draw(streams_of[8], (N_PIPE, EXPERTS * HSPLIT, HE, D // HSPLIT), D ** -0.5, 0.09375, ((0, 16), (1, 32)))
    w_down = bell_draw(streams_of[9], (N_PIPE, EXPERTS * HSPLIT, HE, D // HSPLIT), HE ** -0.5, 0.1875, ((0, 16), (1, 32)))
    return {"act_prev": act_prev, "fwd_routes": fwd_routes, "fwd_gates": fwd_gates, "saved_input": saved_input, "grad_prev": grad_prev, "bwd_routes": bwd_routes, "bwd_gates": bwd_gates, "norm_gain": norm_gain, "w_up": w_up, "w_down": w_down}


def slot_tables(routes, gates, n_experts, capacity):
    rows, picks = routes.shape
    flat = routes.reshape(-1)
    hot = (flat[:, None] == jnp.arange(n_experts, dtype=jnp.int32)[None, :]).astype(jnp.int32)
    before = jnp.cumsum(hot, axis=0) - hot
    place = lax.optimization_barrier(jnp.sum(before * hot, axis=1))
    target = flat * capacity + place
    target_hot = (target[:, None] == jnp.arange(n_experts * capacity, dtype=jnp.int32)[None, :]).astype(jnp.float32)
    target_hot = target_hot.reshape(rows, picks, n_experts * capacity)
    choose = lax.optimization_barrier(jnp.sum(target_hot, axis=1))
    weigh = lax.optimization_barrier(jnp.sum(target_hot * gates[:, :, None], axis=1))
    return (choose, weigh)

def normalize(values, gain):
    scale = lax.rsqrt(lax.optimization_barrier(jnp.mean(values * values, axis=-1, keepdims=True)) + 1e-06)
    return values * scale * gain

def expert_forward(rows, up_rows, down_rows):
    hidden = lax.dot_general(rows, up_rows, (((1,), (1,)), ((), ())), preferred_element_type=jnp.float32)
    active = jax.nn.silu(hidden).astype(jnp.bfloat16)
    return jnp.dot(active, down_rows, preferred_element_type=jnp.float32).astype(jnp.bfloat16)

def expert_backward(rows, cotangent, up_rows, down_rows):
    hidden = lax.dot_general(rows, up_rows, (((1,), (1,)), ((), ())), preferred_element_type=jnp.float32)
    sigma = jax.nn.sigmoid(hidden)
    slope = sigma * (1.0 + hidden * (1.0 - sigma))
    d_active = lax.dot_general(cotangent, down_rows, (((1,), (1,)), ((), ())), preferred_element_type=jnp.float32)
    d_hidden = (d_active * slope).astype(jnp.bfloat16)
    return jnp.dot(d_hidden, up_rows, preferred_element_type=jnp.float32).astype(jnp.bfloat16)

def scatter_rows(choose, values):
    return jnp.einsum('bts,btd->bsd', choose, values.astype(jnp.float32), precision=lax.Precision.HIGHEST)

def gather_rows(weigh, back):
    return jnp.einsum('bts,bsd->btd', weigh, back.astype(jnp.float32), precision=lax.Precision.HIGHEST)

def to_experts(sent):
    blocks = sent.shape[0]
    return sent.reshape(blocks, EXPERTS, CAP, D).transpose(1, 0, 2, 3).reshape(EXPERTS, blocks * CAP, D)

def from_experts(results):
    blocks = N_EXPERT
    return results.reshape(EXPERTS, blocks, CAP, D).transpose(1, 0, 2, 3).reshape(blocks, EXPERTS * CAP, D)

def whole_matrix(blocks):
    return blocks.reshape(EXPERTS, HSPLIT, HE, D // HSPLIT).transpose(0, 2, 1, 3).reshape(EXPERTS, HE, D)

def reference(act_prev, fwd_routes, fwd_gates, saved_input, grad_prev, bwd_routes, bwd_gates, norm_gain, w_up, w_down):
    x_all = jnp.roll(act_prev, 1, axis=0)
    gy_all = jnp.roll(grad_prev, -1, axis=0)
    table_fn = jax.vmap(lambda r, g: slot_tables(r, g, EXPERTS, CAP))

    def section(index):
        gain = norm_gain[index]
        up_all = whole_matrix(w_up[index])
        down_all = whole_matrix(w_down[index])
        x_here = x_all[index].reshape(N_EXPERT, TOK, D)
        choose, weigh = table_fn(fwd_routes[index].reshape(N_EXPERT, TOK, TOPK), fwd_gates[index].reshape(N_EXPERT, TOK, TOPK))
        normed = normalize(x_here.astype(jnp.float32), gain).astype(jnp.bfloat16)
        sent = scatter_rows(choose, normed).astype(jnp.bfloat16)
        grouped = to_experts(sent)
        results = lax.map(lambda item: expert_forward(item[0], item[1], item[2]), (grouped, up_all, down_all))
        back = from_experts(results)
        out_here = (x_here.astype(jnp.float32) + gather_rows(weigh, back)).astype(jnp.bfloat16)
        saved = saved_input[index].reshape(N_EXPERT, TOK, D).astype(jnp.float32)
        gy_here = gy_all[index].reshape(N_EXPERT, TOK, D)
        choose_b, weigh_b = table_fn(bwd_routes[index].reshape(N_EXPERT, TOK, TOPK), bwd_gates[index].reshape(N_EXPERT, TOK, TOPK))
        normed_b = normalize(saved, gain).astype(jnp.bfloat16)
        sent_rows = scatter_rows(choose_b, normed_b).astype(jnp.bfloat16)
        sent_cot = jnp.einsum('bts,btd->bsd', weigh_b, gy_here.astype(jnp.float32), precision=lax.Precision.HIGHEST).astype(jnp.bfloat16)
        grads = lax.map(lambda item: expert_backward(item[0], item[1], item[2], item[3]), (to_experts(sent_rows), to_experts(sent_cot), up_all, down_all))
        d_normed = gather_rows(choose_b, from_experts(grads))
        flat_saved = saved.reshape(TOKENS, D)
        _, pull = jax.vjp(lambda v: normalize(v, gain), flat_saved)
        d_input = pull(d_normed.reshape(TOKENS, D))[0]
        grad_here = (gy_here.reshape(TOKENS, D).astype(jnp.float32) + d_input).astype(jnp.bfloat16)
        return (out_here.reshape(TOKENS, D), grad_here)
    section_out, input_grad = lax.map(section, jnp.arange(N_PIPE, dtype=jnp.int32))
    return (section_out, input_grad)
```

```python
import functools

import jax
import jax.numpy as jnp
from jax import lax
from jax.experimental import pallas as pl
from jax.experimental.pallas import tpu as pltpu
from jax.sharding import PartitionSpec as P

MESH = pl.DeviceIdType.MESH
EPS = 1e-06
ROWS, COT, FWD = 0, 1, 2
DROW, EOUT = 0, 1
TRANS_RHS = (((1,), (1,)), ((), ()))


def slot_masks(routes, here, n_experts, capacity):
    tokens = routes.shape[0]
    relative = lax.rem(routes - here + n_experts, n_experts).astype(jnp.float32)
    down = lax.broadcasted_iota(jnp.int32, (tokens, tokens), 0)
    across = lax.broadcasted_iota(jnp.int32, (tokens, tokens), 1)
    as_row = jnp.sum(jnp.where(down == across, relative, 0.0), axis=0, keepdims=True)
    same = jnp.where(relative == as_row, 1.0, 0.0)
    rank_col = jnp.sum(jnp.where(across < down, same, 0.0), axis=1, keepdims=True)
    rank_row = jnp.sum(jnp.where(down < across, same, 0.0), axis=0, keepdims=True)
    slots = n_experts * capacity
    target_col = (relative * capacity + rank_col).astype(jnp.int32)
    target_row = (as_row * capacity + rank_row).astype(jnp.int32)
    slot_of_col = lax.broadcasted_iota(jnp.int32, (tokens, slots), 1)
    slot_of_row = lax.broadcasted_iota(jnp.int32, (slots, tokens), 0)
    gather = jnp.where(target_col == slot_of_col, 1.0, 0.0).astype(jnp.bfloat16)
    pack = jnp.where(target_row == slot_of_row, 1.0, 0.0).astype(jnp.bfloat16)
    return gather, pack


def kernel(
    sizes,
    act_ref,
    fwd_routes_ref,
    fwd_gates_ref,
    saved_ref,
    grad_ref,
    bwd_routes_ref,
    bwd_gates_ref,
    gain_ref,
    up_ref,
    down_ref,
    out_ref,
    dx_ref,
    x_buf,
    gy_buf,
    up_all,
    down_all,
    normed,
    snd,
    rcv,
    ret,
    bak,
    hid,
    dact,
    mid,
    dn,
    pipe_send,
    pipe_recv,
    w_send,
    w_recv,
    w_own,
    disp_send,
    disp_recv,
    ret_send,
    ret_recv,
):
    n_pipe, n_experts, n_x, cap, chunks, width = sizes
    tokens = saved_ref.shape[1]
    dim = saved_ref.shape[2]
    per_group = 2 * n_x
    pipe = lax.axis_index("pipe")
    place = lax.axis_index("expert")
    here = place // per_group
    spot = lax.rem(place, per_group)
    my_x, core = spot // 2, lax.rem(spot, 2)

    def spot_of(x, c):
        return lax.rem(x + n_x, n_x) * 2 + c

    def group_peer(offset):
        return (pipe, lax.rem(here + offset + n_experts, n_experts) * per_group + spot)

    right = (pipe, here * per_group + spot_of(my_x + 1, core))
    left = (pipe, here * per_group + spot_of(my_x - 1, core))
    sibling = (pipe, here * per_group + spot_of(my_x, 1 - core))
    later = (lax.rem(pipe + 1, n_pipe), place)
    earlier = (lax.rem(pipe + n_pipe - 1, n_pipe), place)

    barrier = pltpu.get_barrier_semaphore()
    peers = [right, left, sibling, later, earlier] + [group_peer(k) for k in range(1, n_experts)]
    for peer in peers:
        pl.semaphore_signal(barrier, inc=1, device_id=peer, device_id_type=MESH)

    def pipe_copy(i):
        src, dst, peer = ((act_ref.at[0], x_buf, later), (grad_ref.at[0], gy_buf, earlier))[i]
        return pltpu.make_async_remote_copy(
            src_ref=src,
            dst_ref=dst,
            send_sem=pipe_send.at[i],
            recv_sem=pipe_recv.at[i],
            device_id=peer,
            device_id_type=MESH,
        )

    def dispatch(which, c, k):
        return pltpu.make_async_remote_copy(
            src_ref=snd.at[which, c, k - 1],
            dst_ref=rcv.at[which, c, k],
            send_sem=disp_send.at[which, c, k - 1],
            recv_sem=disp_recv.at[which, c, k - 1],
            device_id=group_peer(k),
            device_id_type=MESH,
        )

    def give_back(which, c, k):
        return pltpu.make_async_remote_copy(
            src_ref=ret.at[which, c, k - 1],
            dst_ref=bak.at[which, c, k],
            send_sem=ret_send.at[which, c, k - 1],
            recv_sem=ret_recv.at[which, c, k - 1],
            device_id=group_peer(-k),
            device_id_type=MESH,
        )

    half = up_ref.shape[2] // 2
    first, second = pl.ds(0, half), pl.ds(half, half)
    spot_l, spot_r = spot_of(my_x - 1, core), spot_of(my_x + 1, core)
    spot_a = spot_of(my_x + 2, core)
    arrivals = [
        (spot_l, first),
        (spot_l, second),
        (spot_r, first),
        (spot_r, second),
        (spot_a, first),
        (spot_a, second),
    ]

    def weight_copy(m, i):
        own, everything = ((up_ref, up_all), (down_ref, down_all))[m]
        if i < 4:
            rows = (first, second)[i % 2]
            src, dst = own.at[0, 0, rows], everything.at[spot, rows]
            peer = right if i < 2 else left
        elif i == 4:
            src = dst = everything.at[spot_l, first]
            peer = right
        elif i == 5:
            src = dst = everything.at[spot_r, second]
            peer = left
        elif i == 6:
            src, dst, peer = own.at[0, 0], everything.at[spot], sibling
        else:
            at, rows = arrivals[i - 7]
            src = dst = everything.at[at, rows]
            peer = sibling
        return pltpu.make_async_remote_copy(
            src_ref=src,
            dst_ref=dst,
            send_sem=w_send.at[m, i],
            recv_sem=w_recv.at[m, i],
            device_id=peer,
            device_id_type=MESH,
        )

    own_copies = [
        pltpu.make_async_copy(up_ref.at[0, 0], up_all.at[spot], w_own.at[0]),
        pltpu.make_async_copy(down_ref.at[0, 0], down_all.at[spot], w_own.at[1]),
    ]
    for copy in own_copies:
        copy.start()

    def cols(h):
        return pl.ds(pl.multiple_of(h * width, width), width)

    def put_slots(c, low, high, remote, local):
        for k in range(n_experts):
            rows = slice(k * cap, (k + 1) * cap)
            piece = jnp.concatenate([low[rows], high[rows]], axis=0).astype(jnp.bfloat16)
            if k == 0:
                local[c, 0] = piece
            else:
                remote[c, k - 1] = piece

    def take_slots(buf, c):
        whole = [buf[c, k].astype(jnp.float32) for k in range(n_experts)]
        return [
            jnp.concatenate([w[j * cap : (j + 1) * cap] for w in whole], axis=0).astype(jnp.bfloat16)
            for j in range(2)
        ]

    def pack_piece(which, c, pack):
        low, high = [
            jnp.dot(pack, normed[:, cols(2 * c + j)], preferred_element_type=jnp.float32)
            for j in range(2)
        ]
        put_slots(c, low, high, snd.at[which], rcv.at[which])

    def send_piece(which, c):
        for k in range(1, n_experts):
            dispatch(which, c, k).start()

    def pack_and_send(which, pack):
        @pl.loop(0, chunks)
        def _(c):
            pack_piece(which, c, pack)
            send_piece(which, c)

    def scale_of(values):
        return lax.rsqrt(jnp.sum(values * values, axis=-1, keepdims=True) * (1.0 / dim) + EPS)

    gain = gain_ref[...]

    saved = saved_ref[0].astype(jnp.float32)
    scale_b = scale_of(saved)
    normed[...] = (saved * scale_b * gain).astype(jnp.bfloat16)
    gather_b, pack_b = slot_masks(bwd_routes_ref[0], here, n_experts, cap)

    @pl.loop(0, chunks)
    def _(c):
        pack_piece(ROWS, c, pack_b)

    pl.semaphore_wait(barrier, len(peers))

    pipe_copy(1).start()
    pipe_copy(0).start()

    @pl.loop(0, chunks)
    def _(c):
        send_piece(ROWS, c)

    for m in range(2):
        for i in (0, 3, 1, 2, 6):
            weight_copy(m, i).start()

    pipe_copy(1).wait_recv()
    normed[...] = (gy_buf[...].astype(jnp.float32) * bwd_gates_ref[0]).astype(jnp.bfloat16)
    pack_and_send(COT, pack_b)

    gather_f, pack_f = slot_masks(fwd_routes_ref[0], here, n_experts, cap)
    pipe_copy(0).wait_recv()
    x = x_buf[...].astype(jnp.float32)
    normed[...] = (x * scale_of(x) * gain).astype(jnp.bfloat16)
    pack_and_send(FWD, pack_f)

    def pass_on(m):
        weight_copy(m, 0).wait_recv()
        weight_copy(m, 4).start()
        weight_copy(m, 7).start()
        weight_copy(m, 3).wait_recv()
        weight_copy(m, 5).start()
        weight_copy(m, 10).start()
        for i in (1, 2, 4, 5):
            weight_copy(m, i).wait_recv()
            weight_copy(m, 7 + i).start()

    def have_weights(m):
        own_copies[m].wait()
        for i in range(6, 13):
            weight_copy(m, i).wait_recv()

    def into_hidden(which, weights, total):
        total[...] = jnp.zeros_like(total)

        @pl.loop(0, chunks)
        def _(c):
            for k in range(1, n_experts):
                dispatch(which, c, k).wait_recv()
            for j, rows in enumerate(take_slots(rcv.at[which], c)):
                total[...] += lax.dot_general(
                    rows, weights[2 * c + j], TRANS_RHS, preferred_element_type=jnp.float32
                )

    def out_of_hidden(which, weights):
        @pl.loop(0, chunks)
        def _(c):
            low, high = [
                jnp.dot(mid[...], weights[2 * c + j], preferred_element_type=jnp.float32)
                for j in range(2)
            ]
            put_slots(c, low, high, ret.at[which], bak.at[which])
            for k in range(1, n_experts):
                give_back(which, c, k).start()

    pass_on(0)
    have_weights(0)
    into_hidden(ROWS, up_all, hid)
    pass_on(1)
    have_weights(1)
    into_hidden(COT, down_all, dact)
    h = hid[...]
    sigma = 1.0 / (1.0 + jnp.exp(-h))
    mid[...] = (dact[...] * (sigma * (1.0 + h * (1.0 - sigma)))).astype(jnp.bfloat16)
    out_of_hidden(DROW, up_all)

    into_hidden(FWD, up_all, hid)
    h = hid[...]
    mid[...] = (h / (1.0 + jnp.exp(-h))).astype(jnp.bfloat16)
    out_of_hidden(EOUT, down_all)

    def from_slots(which, c, gather):
        for k in range(1, n_experts):
            give_back(which, c, k).wait_recv()
        return [
            jnp.dot(gather, rows, preferred_element_type=jnp.float32)
            for rows in take_slots(bak.at[which], c)
        ]

    def gradient_piece(c, total):
        for j, d in enumerate(from_slots(DROW, c, gather_b)):
            at = cols(2 * c + j)
            scaled = d * gain_ref[:, at]
            dn[:, at] = scaled
            total = total + jnp.sum(
                scaled * saved_ref[0, :, at].astype(jnp.float32), axis=-1, keepdims=True
            )
        return total

    total = lax.fori_loop(0, chunks, gradient_piece, jnp.zeros((tokens, 1), jnp.float32))
    pull = total * (1.0 / dim) * scale_b * scale_b * scale_b
    dx_ref[0] = (
        gy_buf[...].astype(jnp.float32)
        + (dn[...] * scale_b - saved_ref[0].astype(jnp.float32) * pull)
    ).astype(jnp.bfloat16)

    gates = fwd_gates_ref[0]

    @pl.loop(0, chunks)
    def _(c):
        for j, e in enumerate(from_slots(EOUT, c, gather_f)):
            at = cols(2 * c + j)
            out_ref[0, :, at] = (x_buf[:, at].astype(jnp.float32) + e * gates).astype(jnp.bfloat16)

    for i in range(2):
        pipe_copy(i).wait_send()
    for m in range(2):
        for i in range(13):
            weight_copy(m, i).wait_send()

    @pl.loop(0, chunks)
    def _(c):
        for k in range(1, n_experts):
            for which in range(3):
                dispatch(which, c, k).wait_send()
            for which in range(2):
                give_back(which, c, k).wait_send()


def local(
    act_prev,
    fwd_routes,
    fwd_gates,
    saved_input,
    grad_prev,
    bwd_routes,
    bwd_gates,
    norm_gain,
    w_up,
    w_down,
):
    n_pipe = lax.axis_size("pipe")
    n_x = 4
    n_experts = lax.axis_size("expert") // (2 * n_x)
    tokens, dim = act_prev.shape[1], act_prev.shape[2]
    hidden, width = w_up.shape[2], w_up.shape[3]
    cap = 3 * tokens // (2 * n_experts)
    blocks = dim // width
    chunks = blocks // 2
    slots = n_experts * cap
    bf16, f32 = jnp.bfloat16, jnp.float32
    dma = pltpu.SemaphoreType.DMA
    vmem, anywhere = pl.BlockSpec(memory_space=pltpu.VMEM), pl.BlockSpec(memory_space=pl.ANY)
    return pl.pallas_call(
        functools.partial(kernel, (n_pipe, n_experts, n_x, cap, chunks, width)),
        out_shape=[jax.ShapeDtypeStruct(act_prev.shape, bf16)] * 2,
        in_specs=[anywhere, vmem, vmem, vmem, anywhere, vmem, vmem, vmem, anywhere, anywhere],
        out_specs=[vmem, vmem],
        scratch_shapes=[
            pltpu.VMEM((tokens, dim), bf16),
            pltpu.VMEM((tokens, dim), bf16),
            pltpu.VMEM((blocks, hidden, width), bf16),
            pltpu.VMEM((blocks, hidden, width), bf16),
            pltpu.VMEM((tokens, dim), bf16),
            pltpu.VMEM((3, chunks, n_experts - 1, 2 * cap, width), bf16),
            pltpu.VMEM((3, chunks, n_experts, 2 * cap, width), bf16),
            pltpu.VMEM((2, chunks, n_experts - 1, 2 * cap, width), bf16),
            pltpu.VMEM((2, chunks, n_experts, 2 * cap, width), bf16),
            pltpu.VMEM((slots, hidden), f32),
            pltpu.VMEM((slots, hidden), f32),
            pltpu.VMEM((slots, hidden), bf16),
            pltpu.VMEM((tokens, dim), f32),
            dma((2,)),
            dma((2,)),
            dma((2, 13)),
            dma((2, 13)),
            dma((2,)),
            dma((3, chunks, n_experts - 1)),
            dma((3, chunks, n_experts - 1)),
            dma((2, chunks, n_experts - 1)),
            dma((2, chunks, n_experts - 1)),
        ],
        compiler_params=pltpu.CompilerParams(
            collective_id=0, has_side_effects=True, vmem_limit_bytes=48 * 2**20
        ),
        cost_estimate=pl.CostEstimate(
            flops=10 * slots * hidden * dim, bytes_accessed=24 * 2**20, transcendentals=0
        ),
    )(
        act_prev,
        fwd_routes,
        fwd_gates,
        saved_input,
        grad_prev,
        bwd_routes,
        bwd_gates,
        norm_gain,
        w_up,
        w_down,
    )


def solution(mesh):
    rows = P("pipe", "expert", None)
    blocks = P("pipe", "expert", None, None)
    return jax.shard_map(
        local,
        mesh=mesh,
        in_specs=(rows,) * 7 + (P("pipe", None), blocks, blocks),
        out_specs=(rows, rows),
        check_vma=False,
    )
```

```python
import functools

import jax
import jax.numpy as jnp
from jax import lax
from jax.experimental import pallas as pl
from jax.experimental.pallas import tpu as pltpu
from jax.sharding import PartitionSpec as P

MESH = pl.DeviceIdType.MESH
EPS = 1e-06
ROWS, COT, FWD = 0, 1, 2
DROW, EOUT = 0, 1
TRANS_RHS = (((1,), (1,)), ((), ()))


def as_column(row):
    n = row.shape[1]
    down = lax.broadcasted_iota(jnp.int32, (n, n), 0)
    across = lax.broadcasted_iota(jnp.int32, (n, n), 1)
    return jnp.sum(jnp.where(down == across, row, 0.0), axis=1, keepdims=True)


def slot_masks(routes, here, n_experts, capacity):
    tokens = routes.shape[1]
    as_row = lax.rem(routes - here + n_experts, n_experts).astype(jnp.float32)
    relative = as_column(as_row)
    down = lax.broadcasted_iota(jnp.int32, (tokens, tokens), 0)
    across = lax.broadcasted_iota(jnp.int32, (tokens, tokens), 1)
    same = jnp.where(relative == as_row, 1.0, 0.0)
    rank_col = jnp.sum(jnp.where(across < down, same, 0.0), axis=1, keepdims=True)
    rank_row = jnp.sum(jnp.where(down < across, same, 0.0), axis=0, keepdims=True)
    slots = n_experts * capacity
    target_col = (relative * capacity + rank_col).astype(jnp.int32)
    target_row = (as_row * capacity + rank_row).astype(jnp.int32)
    slot_of_col = lax.broadcasted_iota(jnp.int32, (tokens, slots), 1)
    slot_of_row = lax.broadcasted_iota(jnp.int32, (slots, tokens), 0)
    gather = jnp.where(target_col == slot_of_col, 1.0, 0.0).astype(jnp.bfloat16)
    pack = jnp.where(target_row == slot_of_row, 1.0, 0.0).astype(jnp.bfloat16)
    return gather, pack


def kernel(
    sizes,
    act_ref,
    fwd_routes_hbm,
    fwd_gates_hbm,
    saved_hbm,
    grad_ref,
    bwd_routes_hbm,
    bwd_gates_hbm,
    gain_hbm,
    up_ref,
    down_ref,
    out_ref,
    dx_ref,
    fwd_routes_ref,
    fwd_gates_ref,
    saved_ref,
    bwd_routes_ref,
    bwd_gates_ref,
    gain_ref,
    x_buf,
    gy_buf,
    passing,
    up_all,
    down_all,
    normed,
    snd,
    rcv,
    ret,
    bak,
    hid,
    dact,
    mid,
    dn,
    load_sem,
    pipe_send,
    pipe_recv,
    relay_send,
    relay_recv,
    w_send,
    w_recv,
    w_own,
    disp_send,
    disp_recv,
    ret_send,
    ret_recv,
):
    n_pipe, n_y, n_experts, n_x, cap, chunks, width = sizes
    tokens = saved_ref.shape[1]
    dim = saved_ref.shape[2]
    per_group = 2 * n_x
    pipe = lax.axis_index("pipe")
    place = lax.axis_index("expert")
    here = place // per_group
    spot = lax.rem(place, per_group)
    my_x, core = spot // 2, lax.rem(spot, 2)

    def spot_of(x, c):
        return lax.rem(x + n_x, n_x) * 2 + c

    def group_peer(offset):
        return (pipe, lax.rem(here + offset + n_experts, n_experts) * per_group + spot)

    right = (pipe, here * per_group + spot_of(my_x + 1, core))
    left = (pipe, here * per_group + spot_of(my_x - 1, core))
    sibling = (pipe, here * per_group + spot_of(my_x, 1 - core))
    later = (lax.rem(pipe + 1, n_pipe), place)
    earlier = (lax.rem(pipe + n_pipe - 1, n_pipe), place)
    my_y, my_z = lax.rem(pipe, n_y), pipe // n_y
    n_z = n_pipe // n_y

    def at_yz(y, z):
        return (lax.rem(z + n_z, n_z) * n_y + y, place)

    barrier = pltpu.get_barrier_semaphore()

    def greet(peer):
        pl.semaphore_signal(barrier, inc=1, device_id=peer, device_id_type=MESH)

    for k in range(1, n_experts):
        greet(group_peer(k))
    for peer in (right, left, sibling):
        greet(peer)
    for k in range(1, n_y):
        greet(at_yz(lax.rem(my_y + k, n_y), my_z))

    @pl.when(my_y == 0)
    def _():
        for y in range(n_y):
            greet(at_yz(y, my_z - 1))

    @pl.when(my_y == n_y - 1)
    def _():
        for y in range(n_y):
            greet(at_yz(y, my_z + 1))

    greetings = (n_experts - 1) + 3 + (n_y - 1) + 2

    loads = [
        pltpu.make_async_copy(src, dst, load_sem.at[i])
        for i, (src, dst) in enumerate(
            (
                (saved_hbm, saved_ref),
                (gain_hbm, gain_ref),
                (bwd_routes_hbm, bwd_routes_ref),
                (bwd_gates_hbm, bwd_gates_ref),
                (fwd_routes_hbm, fwd_routes_ref),
                (fwd_gates_hbm, fwd_gates_ref),
            )
        )
    ]
    for load in loads:
        load.start()

    part = tokens // n_y
    last_y = n_y - 1
    crossing = (my_y == last_y, my_y == 0)
    straight = (last_y, 0)
    relays = (range(0, last_y), range(1, n_y))

    def part_rows(y):
        return pl.ds(y * part, part)

    def remote(src, dst, send_sem, recv_sem, peer):
        return pltpu.make_async_remote_copy(
            src_ref=src,
            dst_ref=dst,
            send_sem=send_sem,
            recv_sem=recv_sem,
            device_id=peer,
            device_id_type=MESH,
        )

    pipe_ends = ((act_ref, x_buf, later), (grad_ref, gy_buf, earlier))

    def pipe_part(w, y):
        src, dst, peer = pipe_ends[w]
        rows = part_rows(y)
        return remote(src.at[0, rows], dst.at[rows], pipe_send.at[w, y], pipe_recv.at[w, y], peer)

    def pipe_to_relay(w, y):
        src = pipe_ends[w][0].at[0, part_rows(y)]
        return remote(src, passing.at[w], pipe_send.at[w, y], relay_recv.at[w], at_yz(y, my_z))

    def pipe_from_relay(w, y):
        peer = (at_yz(0, my_z + 1), at_yz(last_y, my_z - 1))[w]
        dst = pipe_ends[w][1].at[part_rows(y)]
        return remote(passing.at[w], dst, relay_send.at[w], pipe_recv.at[w, y], peer)

    def pipe_start(w):
        @pl.when(crossing[w])
        def _():
            for y in relays[w]:
                pipe_to_relay(w, y).start()
            pipe_part(w, straight[w]).start()

        @pl.when(jnp.logical_not(crossing[w]))
        def _():
            for y in range(n_y):
                pipe_part(w, y).start()

    def pipe_pass_on(w):
        for y in relays[w]:

            @pl.when(my_y == y)
            def _():
                pipe_to_relay(w, y).wait_recv()
                pipe_from_relay(w, y).start()

    def pipe_arrived(w):
        for y in range(n_y):
            pipe_part(w, y).wait_recv()

    def pipe_sent(w):
        for y in range(n_y):
            pipe_part(w, y).wait_send()
        for y in relays[w]:

            @pl.when(my_y == y)
            def _():
                pipe_from_relay(w, y).wait_send()

    def dispatch(which, c, k):
        return pltpu.make_async_remote_copy(
            src_ref=snd.at[which, c, k - 1],
            dst_ref=rcv.at[which, c, k],
            send_sem=disp_send.at[which, c, k - 1],
            recv_sem=disp_recv.at[which, c, k - 1],
            device_id=group_peer(k),
            device_id_type=MESH,
        )

    def give_back(which, c, k):
        return pltpu.make_async_remote_copy(
            src_ref=ret.at[which, c, k - 1],
            dst_ref=bak.at[which, c, k],
            send_sem=ret_send.at[which, c, k - 1],
            recv_sem=ret_recv.at[which, c, k - 1],
            device_id=group_peer(-k),
            device_id_type=MESH,
        )

    half = up_ref.shape[2] // 2
    first, second = pl.ds(0, half), pl.ds(half, half)
    spot_l, spot_r = spot_of(my_x - 1, core), spot_of(my_x + 1, core)
    spot_a = spot_of(my_x + 2, core)
    arrivals = [
        (spot_l, first),
        (spot_l, second),
        (spot_r, first),
        (spot_r, second),
        (spot_a, first),
        (spot_a, second),
    ]

    def weight_copy(m, i):
        own, everything = ((up_ref, up_all), (down_ref, down_all))[m]
        if i < 4:
            rows = (first, second)[i % 2]
            src, dst = own.at[0, 0, rows], everything.at[spot, rows]
            peer = right if i < 2 else left
        elif i == 4:
            src = dst = everything.at[spot_l, first]
            peer = right
        elif i == 5:
            src = dst = everything.at[spot_r, second]
            peer = left
        elif i == 6:
            src, dst, peer = own.at[0, 0], everything.at[spot], sibling
        else:
            at, rows = arrivals[i - 7]
            src = dst = everything.at[at, rows]
            peer = sibling
        return pltpu.make_async_remote_copy(
            src_ref=src,
            dst_ref=dst,
            send_sem=w_send.at[m, i],
            recv_sem=w_recv.at[m, i],
            device_id=peer,
            device_id_type=MESH,
        )

    own_copies = [
        pltpu.make_async_copy(up_ref.at[0, 0], up_all.at[spot], w_own.at[0]),
        pltpu.make_async_copy(down_ref.at[0, 0], down_all.at[spot], w_own.at[1]),
    ]
    for copy in own_copies:
        copy.start()

    def cols(h):
        return pl.ds(pl.multiple_of(h * width, width), width)

    def put_slots(c, low, high, remote, local):
        for k in range(n_experts):
            rows = slice(k * cap, (k + 1) * cap)
            piece = jnp.concatenate([low[rows], high[rows]], axis=0).astype(jnp.bfloat16)
            if k == 0:
                local[c, 0] = piece
            else:
                remote[c, k - 1] = piece

    def take_slots(buf, c):
        whole = [buf[c, k].astype(jnp.float32) for k in range(n_experts)]
        return [
            jnp.concatenate([w[j * cap : (j + 1) * cap] for w in whole], axis=0).astype(jnp.bfloat16)
            for j in range(2)
        ]

    def pack_piece(which, c, pack):
        low, high = [
            jnp.dot(pack, normed[:, cols(2 * c + j)], preferred_element_type=jnp.float32)
            for j in range(2)
        ]
        put_slots(c, low, high, snd.at[which], rcv.at[which])

    def send_piece(which, c):
        for k in range(1, n_experts):
            dispatch(which, c, k).start()

    def scale_of(values):
        return lax.rsqrt(jnp.sum(values * values, axis=-1, keepdims=True) * (1.0 / dim) + EPS)

    for load in loads:
        load.wait()
    gain = gain_ref[...]
    saved = saved_ref[0].astype(jnp.float32)
    scale_b = scale_of(saved)
    normed[...] = (saved * scale_b * gain).astype(jnp.bfloat16)
    gather_b, pack_b = slot_masks(bwd_routes_ref[...], here, n_experts, cap)

    @pl.loop(0, chunks)
    def _(c):
        pack_piece(ROWS, c, pack_b)

    pl.semaphore_wait(barrier, greetings)

    pipe_start(1)
    pipe_start(0)

    @pl.loop(0, chunks)
    def _(c):
        send_piece(ROWS, c)

    pipe_pass_on(1)
    pipe_pass_on(0)

    for m in range(2):
        for i in (0, 3, 1, 2, 6):
            weight_copy(m, i).start()

    gates_b = as_column(bwd_gates_ref[...])
    pipe_arrived(1)
    normed[...] = (gy_buf[...].astype(jnp.float32) * gates_b).astype(jnp.bfloat16)

    @pl.loop(0, chunks)
    def _(c):
        pack_piece(COT, c, pack_b)
        send_piece(COT, c)

    gather_f, pack_f = slot_masks(fwd_routes_ref[...], here, n_experts, cap)
    pipe_arrived(0)
    x = x_buf[...].astype(jnp.float32)
    normed[...] = (x * scale_of(x) * gain).astype(jnp.bfloat16)

    @pl.loop(0, chunks)
    def _(c):
        pack_piece(FWD, c, pack_f)
        send_piece(FWD, c)

    def pass_on(m):
        weight_copy(m, 0).wait_recv()
        weight_copy(m, 4).start()
        weight_copy(m, 7).start()
        weight_copy(m, 3).wait_recv()
        weight_copy(m, 5).start()
        weight_copy(m, 10).start()
        for i in (1, 2, 4, 5):
            weight_copy(m, i).wait_recv()
            weight_copy(m, 7 + i).start()

    def have_weights(m):
        own_copies[m].wait()
        for i in range(6, 13):
            weight_copy(m, i).wait_recv()

    def into_hidden(which, weights, total):
        total[...] = jnp.zeros_like(total)

        @pl.loop(0, chunks)
        def _(c):
            for k in range(1, n_experts):
                dispatch(which, c, k).wait_recv()
            for j, rows in enumerate(take_slots(rcv.at[which], c)):
                total[...] += lax.dot_general(
                    rows, weights[2 * c + j], TRANS_RHS, preferred_element_type=jnp.float32
                )

    def out_of_hidden(which, weights):
        @pl.loop(0, chunks)
        def _(c):
            low, high = [
                jnp.dot(mid[...], weights[2 * c + j], preferred_element_type=jnp.float32)
                for j in range(2)
            ]
            put_slots(c, low, high, ret.at[which], bak.at[which])
            for k in range(1, n_experts):
                give_back(which, c, k).start()

    pass_on(0)
    have_weights(0)
    into_hidden(ROWS, up_all, hid)
    pass_on(1)
    have_weights(1)
    into_hidden(COT, down_all, dact)
    h = hid[...]
    sigma = 1.0 / (1.0 + jnp.exp(-h))
    mid[...] = (dact[...] * (sigma * (1.0 + h * (1.0 - sigma)))).astype(jnp.bfloat16)
    out_of_hidden(DROW, up_all)

    into_hidden(FWD, up_all, hid)
    h = hid[...]
    mid[...] = (h / (1.0 + jnp.exp(-h))).astype(jnp.bfloat16)
    out_of_hidden(EOUT, down_all)

    def from_slots(which, c, gather):
        for k in range(1, n_experts):
            give_back(which, c, k).wait_recv()
        return [
            jnp.dot(gather, rows, preferred_element_type=jnp.float32)
            for rows in take_slots(bak.at[which], c)
        ]

    def gradient_piece(c, total):
        for j, d in enumerate(from_slots(DROW, c, gather_b)):
            at = cols(2 * c + j)
            scaled = d * gain_ref[:, at]
            dn[:, at] = scaled
            total = total + jnp.sum(
                scaled * saved_ref[0, :, at].astype(jnp.float32), axis=-1, keepdims=True
            )
        return total

    total = lax.fori_loop(0, chunks, gradient_piece, jnp.zeros((tokens, 1), jnp.float32))
    pull = total * (1.0 / dim) * scale_b * scale_b * scale_b
    dx_ref[0] = (
        gy_buf[...].astype(jnp.float32)
        + (dn[...] * scale_b - saved_ref[0].astype(jnp.float32) * pull)
    ).astype(jnp.bfloat16)

    gates = as_column(fwd_gates_ref[...])

    @pl.loop(0, chunks)
    def _(c):
        for j, e in enumerate(from_slots(EOUT, c, gather_f)):
            at = cols(2 * c + j)
            out_ref[0, :, at] = (x_buf[:, at].astype(jnp.float32) + e * gates).astype(jnp.bfloat16)

    for w in range(2):
        pipe_sent(w)
    for m in range(2):
        for i in range(13):
            weight_copy(m, i).wait_send()

    @pl.loop(0, chunks)
    def _(c):
        for k in range(1, n_experts):
            for which in range(3):
                dispatch(which, c, k).wait_send()
            for which in range(2):
                give_back(which, c, k).wait_send()


def local(
    act_prev,
    fwd_routes,
    fwd_gates,
    saved_input,
    grad_prev,
    bwd_routes,
    bwd_gates,
    norm_gain,
    w_up,
    w_down,
):
    n_pipe = lax.axis_size("pipe")
    n_x, n_y = 4, 4
    n_experts = lax.axis_size("expert") // (2 * n_x)
    tokens, dim = act_prev.shape[1], act_prev.shape[2]
    hidden, width = w_up.shape[2], w_up.shape[3]
    cap = 3 * tokens // (2 * n_experts)
    blocks = dim // width
    chunks = blocks // 2
    slots = n_experts * cap
    bf16, f32 = jnp.bfloat16, jnp.float32
    dma = pltpu.SemaphoreType.DMA
    vmem, hbm = pl.BlockSpec(memory_space=pltpu.VMEM), pl.BlockSpec(memory_space=pltpu.HBM)
    return pl.pallas_call(
        functools.partial(kernel, (n_pipe, n_y, n_experts, n_x, cap, chunks, width)),
        out_shape=[jax.ShapeDtypeStruct(act_prev.shape, bf16)] * 2,
        in_specs=[hbm] * 10,
        out_specs=[vmem, vmem],
        scratch_shapes=[
            pltpu.VMEM((1, tokens), jnp.int32),
            pltpu.VMEM((1, tokens), f32),
            pltpu.VMEM((1, tokens, dim), bf16),
            pltpu.VMEM((1, tokens), jnp.int32),
            pltpu.VMEM((1, tokens), f32),
            pltpu.VMEM((1, dim), f32),
            pltpu.VMEM((tokens, dim), bf16),
            pltpu.VMEM((tokens, dim), bf16),
            pltpu.VMEM((2, tokens // n_y, dim), bf16),
            pltpu.VMEM((blocks, hidden, width), bf16),
            pltpu.VMEM((blocks, hidden, width), bf16),
            pltpu.VMEM((tokens, dim), bf16),
            pltpu.VMEM((3, chunks, n_experts - 1, 2 * cap, width), bf16),
            pltpu.VMEM((3, chunks, n_experts, 2 * cap, width), bf16),
            pltpu.VMEM((2, chunks, n_experts - 1, 2 * cap, width), bf16),
            pltpu.VMEM((2, chunks, n_experts, 2 * cap, width), bf16),
            pltpu.VMEM((slots, hidden), f32),
            pltpu.VMEM((slots, hidden), f32),
            pltpu.VMEM((slots, hidden), bf16),
            pltpu.VMEM((tokens, dim), f32),
            dma((6,)),
            dma((2, n_y)),
            dma((2, n_y)),
            dma((2,)),
            dma((2,)),
            dma((2, 13)),
            dma((2, 13)),
            dma((2,)),
            dma((3, chunks, n_experts - 1)),
            dma((3, chunks, n_experts - 1)),
            dma((2, chunks, n_experts - 1)),
            dma((2, chunks, n_experts - 1)),
        ],
        compiler_params=pltpu.CompilerParams(
            collective_id=0, has_side_effects=True, vmem_limit_bytes=60 * 2**20
        ),
        cost_estimate=pl.CostEstimate(
            flops=10 * slots * hidden * dim, bytes_accessed=24 * 2**20, transcendentals=0
        ),
    )(
        act_prev,
        fwd_routes.reshape(1, tokens),
        fwd_gates.reshape(1, tokens),
        saved_input,
        grad_prev,
        bwd_routes.reshape(1, tokens),
        bwd_gates.reshape(1, tokens),
        norm_gain,
        w_up,
        w_down,
    )


def solution(mesh):
    rows = P("pipe", "expert", None)
    blocks = P("pipe", "expert", None, None)
    return jax.shard_map(
        local,
        mesh=mesh,
        in_specs=(rows,) * 7 + (P("pipe", None), blocks, blocks),
        out_specs=(rows, rows),
        check_vma=False,
    )
```

```python
import functools

import jax
import jax.numpy as jnp
from jax import lax
from jax.experimental import pallas as pl
from jax.experimental.pallas import tpu as pltpu
from jax.sharding import PartitionSpec as P

MESH = pl.DeviceIdType.MESH
EPS = 1e-06
ROWS, COT, FWD = 0, 1, 2
DROW, EOUT = 0, 1
TRANS_RHS = (((1,), (1,)), ((), ()))


def as_column(row):
    n = row.shape[1]
    down = lax.broadcasted_iota(jnp.int32, (n, n), 0)
    across = lax.broadcasted_iota(jnp.int32, (n, n), 1)
    return jnp.sum(jnp.where(down == across, row, 0.0), axis=1, keepdims=True)


def slot_masks(routes, here, n_experts, capacity):
    tokens = routes.shape[1]
    as_row = lax.rem(routes - here + n_experts, n_experts).astype(jnp.float32)
    relative = as_column(as_row)
    down = lax.broadcasted_iota(jnp.int32, (tokens, tokens), 0)
    across = lax.broadcasted_iota(jnp.int32, (tokens, tokens), 1)
    same = jnp.where(relative == as_row, 1.0, 0.0)
    rank_col = jnp.sum(jnp.where(across < down, same, 0.0), axis=1, keepdims=True)
    rank_row = jnp.sum(jnp.where(down < across, same, 0.0), axis=0, keepdims=True)
    slots = n_experts * capacity
    target_col = (relative * capacity + rank_col).astype(jnp.int32)
    target_row = (as_row * capacity + rank_row).astype(jnp.int32)
    slot_of_col = lax.broadcasted_iota(jnp.int32, (tokens, slots), 1)
    slot_of_row = lax.broadcasted_iota(jnp.int32, (slots, tokens), 0)
    gather = jnp.where(target_col == slot_of_col, 1.0, 0.0).astype(jnp.bfloat16)
    pack = jnp.where(target_row == slot_of_row, 1.0, 0.0).astype(jnp.bfloat16)
    return gather, pack


def kernel(
    sizes,
    act_ref,
    fwd_routes_hbm,
    fwd_gates_hbm,
    saved_hbm,
    grad_ref,
    bwd_routes_hbm,
    bwd_gates_hbm,
    gain_hbm,
    up_ref,
    down_ref,
    out_ref,
    dx_ref,
    fwd_routes_ref,
    fwd_gates_ref,
    saved_ref,
    bwd_routes_ref,
    bwd_gates_ref,
    gain_ref,
    x_buf,
    gy_buf,
    passing,
    up_all,
    down_all,
    normed,
    snd,
    rcv,
    ret,
    bak,
    hid,
    dact,
    mid,
    dn,
    load_sem,
    pipe_send,
    pipe_recv,
    relay_send,
    relay_recv,
    w_send,
    w_recv,
    w_own,
    disp_send,
    disp_recv,
    ret_send,
    ret_recv,
):
    n_pipe, n_y, n_experts, n_x, cap, chunks, width = sizes
    tokens = saved_ref.shape[1]
    dim = saved_ref.shape[2]
    per_group = 2 * n_x
    pipe = lax.axis_index("pipe")
    place = lax.axis_index("expert")
    here = place // per_group
    spot = lax.rem(place, per_group)
    my_x, core = spot // 2, lax.rem(spot, 2)

    def spot_of(x, c):
        return lax.rem(x + n_x, n_x) * 2 + c

    def group_peer(offset):
        return (pipe, lax.rem(here + offset + n_experts, n_experts) * per_group + spot)

    right = (pipe, here * per_group + spot_of(my_x + 1, core))
    left = (pipe, here * per_group + spot_of(my_x - 1, core))
    sibling = (pipe, here * per_group + spot_of(my_x, 1 - core))
    later = (lax.rem(pipe + 1, n_pipe), place)
    earlier = (lax.rem(pipe + n_pipe - 1, n_pipe), place)
    my_y, my_z = lax.rem(pipe, n_y), pipe // n_y
    n_z = n_pipe // n_y

    def at_yz(y, z):
        return (lax.rem(z + n_z, n_z) * n_y + y, place)

    barrier = pltpu.get_barrier_semaphore()

    def greet(peer):
        pl.semaphore_signal(barrier, inc=1, device_id=peer, device_id_type=MESH)

    for k in range(1, n_experts):
        greet(group_peer(k))
    for peer in (right, left, sibling):
        greet(peer)
    for k in range(1, n_y):
        greet(at_yz(lax.rem(my_y + k, n_y), my_z))

    @pl.when(my_y == 0)
    def _():
        for y in range(n_y):
            greet(at_yz(y, my_z - 1))

    @pl.when(my_y == n_y - 1)
    def _():
        for y in range(n_y):
            greet(at_yz(y, my_z + 1))

    greetings = (n_experts - 1) + 3 + (n_y - 1) + 2

    loads = [
        pltpu.make_async_copy(src, dst, load_sem.at[i])
        for i, (src, dst) in enumerate(
            (
                (saved_hbm, saved_ref),
                (gain_hbm, gain_ref),
                (bwd_routes_hbm, bwd_routes_ref),
                (bwd_gates_hbm, bwd_gates_ref),
                (fwd_routes_hbm, fwd_routes_ref),
                (fwd_gates_hbm, fwd_gates_ref),
            )
        )
    ]
    for load in loads:
        load.start()

    part = tokens // n_y
    last_y = n_y - 1
    crossing = (my_y == last_y, my_y == 0)
    straight = (last_y, 0)
    relays = (range(0, last_y), range(1, n_y))

    def part_rows(y):
        return pl.ds(y * part, part)

    def remote(src, dst, send_sem, recv_sem, peer):
        return pltpu.make_async_remote_copy(
            src_ref=src,
            dst_ref=dst,
            send_sem=send_sem,
            recv_sem=recv_sem,
            device_id=peer,
            device_id_type=MESH,
        )

    pipe_ends = ((act_ref, x_buf, later), (grad_ref, gy_buf, earlier))

    def pipe_part(w, y):
        src, dst, peer = pipe_ends[w]
        rows = part_rows(y)
        return remote(src.at[0, rows], dst.at[rows], pipe_send.at[w, y], pipe_recv.at[w, y], peer)

    def pipe_to_relay(w, y):
        src = pipe_ends[w][0].at[0, part_rows(y)]
        return remote(src, passing.at[w], pipe_send.at[w, y], relay_recv.at[w], at_yz(y, my_z))

    def pipe_from_relay(w, y):
        peer = (at_yz(0, my_z + 1), at_yz(last_y, my_z - 1))[w]
        dst = pipe_ends[w][1].at[part_rows(y)]
        return remote(passing.at[w], dst, relay_send.at[w], pipe_recv.at[w, y], peer)

    def pipe_start(w):
        @pl.when(crossing[w])
        def _():
            for y in relays[w]:
                pipe_to_relay(w, y).start()
            pipe_part(w, straight[w]).start()

        @pl.when(jnp.logical_not(crossing[w]))
        def _():
            for y in range(n_y):
                pipe_part(w, y).start()

    def pipe_pass_on(w):
        for y in relays[w]:

            @pl.when(my_y == y)
            def _():
                pipe_to_relay(w, y).wait_recv()
                pipe_from_relay(w, y).start()

    def pipe_arrived(w):
        for y in range(n_y):
            pipe_part(w, y).wait_recv()

    def pipe_sent(w):
        for y in range(n_y):
            pipe_part(w, y).wait_send()
        for y in relays[w]:

            @pl.when(my_y == y)
            def _():
                pipe_from_relay(w, y).wait_send()

    def dispatch(which, c, k):
        return pltpu.make_async_remote_copy(
            src_ref=snd.at[which, c, k - 1],
            dst_ref=rcv.at[which, c, k],
            send_sem=disp_send.at[which, c, k - 1],
            recv_sem=disp_recv.at[which, c, k - 1],
            device_id=group_peer(k),
            device_id_type=MESH,
        )

    def give_back(which, c, k):
        return pltpu.make_async_remote_copy(
            src_ref=ret.at[which, c, k - 1],
            dst_ref=bak.at[which, c, k],
            send_sem=ret_send.at[which, c, k - 1],
            recv_sem=ret_recv.at[which, c, k - 1],
            device_id=group_peer(-k),
            device_id_type=MESH,
        )

    half = up_ref.shape[2] // 2
    first, second = pl.ds(0, half), pl.ds(half, half)
    spot_l, spot_r = spot_of(my_x - 1, core), spot_of(my_x + 1, core)
    spot_a = spot_of(my_x + 2, core)
    arrivals = [
        (spot_l, first),
        (spot_l, second),
        (spot_r, first),
        (spot_r, second),
        (spot_a, first),
        (spot_a, second),
    ]

    def weight_copy(m, i):
        own, everything = ((up_ref, up_all), (down_ref, down_all))[m]
        if i < 4:
            rows = (first, second)[i % 2]
            src, dst = own.at[0, 0, rows], everything.at[spot, rows]
            peer = right if i < 2 else left
        elif i == 4:
            src = dst = everything.at[spot_l, first]
            peer = right
        elif i == 5:
            src = dst = everything.at[spot_r, second]
            peer = left
        elif i == 6:
            src, dst, peer = own.at[0, 0], everything.at[spot], sibling
        else:
            at, rows = arrivals[i - 7]
            src = dst = everything.at[at, rows]
            peer = sibling
        return pltpu.make_async_remote_copy(
            src_ref=src,
            dst_ref=dst,
            send_sem=w_send.at[m, i],
            recv_sem=w_recv.at[m, i],
            device_id=peer,
            device_id_type=MESH,
        )

    own_copies = [
        pltpu.make_async_copy(up_ref.at[0, 0], up_all.at[spot], w_own.at[0]),
        pltpu.make_async_copy(down_ref.at[0, 0], down_all.at[spot], w_own.at[1]),
    ]
    for copy in own_copies:
        copy.start()

    def cols(h):
        return pl.ds(pl.multiple_of(h * width, width), width)

    def put_slots(c, low, high, remote, local):
        for k in range(n_experts):
            rows = slice(k * cap, (k + 1) * cap)
            piece = jnp.concatenate([low[rows], high[rows]], axis=0).astype(jnp.bfloat16)
            if k == 0:
                local[c, 0] = piece
            else:
                remote[c, k - 1] = piece

    def take_slots(buf, c):
        whole = [buf[c, k].astype(jnp.float32) for k in range(n_experts)]
        return [
            jnp.concatenate([w[j * cap : (j + 1) * cap] for w in whole], axis=0).astype(jnp.bfloat16)
            for j in range(2)
        ]

    def pack_piece(which, c, pack):
        low, high = [
            jnp.dot(pack, normed[:, cols(2 * c + j)], preferred_element_type=jnp.float32)
            for j in range(2)
        ]
        put_slots(c, low, high, snd.at[which], rcv.at[which])

    def send_piece(which, c):
        for k in range(1, n_experts):
            dispatch(which, c, k).start()

    def scale_of(values):
        return lax.rsqrt(jnp.sum(values * values, axis=-1, keepdims=True) * (1.0 / dim) + EPS)

    for load in loads:
        load.wait()
    gain = gain_ref[...]
    saved = saved_ref[0].astype(jnp.float32)
    scale_b = scale_of(saved)
    normed[...] = (saved * scale_b * gain).astype(jnp.bfloat16)
    gather_b, pack_b = slot_masks(bwd_routes_ref[...], here, n_experts, cap)

    pack_piece(ROWS, 0, pack_b)
    pl.semaphore_wait(barrier, greetings)

    pipe_start(1)
    pipe_start(0)
    send_piece(ROWS, 0)
    for m in range(2):
        for i in (0, 3, 1, 2, 6):
            weight_copy(m, i).start()
    pipe_pass_on(1)

    @pl.loop(1, chunks)
    def _(c):
        pack_piece(ROWS, c, pack_b)
        send_piece(ROWS, c)

    pipe_pass_on(0)


    gates_b = as_column(bwd_gates_ref[...])
    pipe_arrived(1)
    normed[...] = (gy_buf[...].astype(jnp.float32) * gates_b).astype(jnp.bfloat16)

    @pl.loop(0, chunks)
    def _(c):
        pack_piece(COT, c, pack_b)
        send_piece(COT, c)

    gather_f, pack_f = slot_masks(fwd_routes_ref[...], here, n_experts, cap)
    pipe_arrived(0)
    x = x_buf[...].astype(jnp.float32)
    normed[...] = (x * scale_of(x) * gain).astype(jnp.bfloat16)

    @pl.loop(0, chunks)
    def _(c):
        pack_piece(FWD, c, pack_f)
        send_piece(FWD, c)

    def pass_on(m):
        weight_copy(m, 0).wait_recv()
        weight_copy(m, 4).start()
        weight_copy(m, 7).start()
        weight_copy(m, 3).wait_recv()
        weight_copy(m, 5).start()
        weight_copy(m, 10).start()
        for i in (1, 2, 4, 5):
            weight_copy(m, i).wait_recv()
            weight_copy(m, 7 + i).start()

    def have_weights(m):
        own_copies[m].wait()
        for i in range(6, 13):
            weight_copy(m, i).wait_recv()

    def into_hidden(which, weights, total):
        total[...] = jnp.zeros_like(total)

        @pl.loop(0, chunks)
        def _(c):
            for k in range(1, n_experts):
                dispatch(which, c, k).wait_recv()
            for j, rows in enumerate(take_slots(rcv.at[which], c)):
                total[...] += lax.dot_general(
                    rows, weights[2 * c + j], TRANS_RHS, preferred_element_type=jnp.float32
                )

    def out_of_hidden(which, weights):
        @pl.loop(0, chunks)
        def _(c):
            low, high = [
                jnp.dot(mid[...], weights[2 * c + j], preferred_element_type=jnp.float32)
                for j in range(2)
            ]
            put_slots(c, low, high, ret.at[which], bak.at[which])
            for k in range(1, n_experts):
                give_back(which, c, k).start()

    pass_on(0)
    have_weights(0)
    into_hidden(ROWS, up_all, hid)
    pass_on(1)
    have_weights(1)
    into_hidden(COT, down_all, dact)
    h = hid[...]
    sigma = 1.0 / (1.0 + jnp.exp(-h))
    mid[...] = (dact[...] * (sigma * (1.0 + h * (1.0 - sigma)))).astype(jnp.bfloat16)
    out_of_hidden(DROW, up_all)

    into_hidden(FWD, up_all, hid)
    h = hid[...]
    mid[...] = (h / (1.0 + jnp.exp(-h))).astype(jnp.bfloat16)
    out_of_hidden(EOUT, down_all)

    def from_slots(which, c, gather):
        for k in range(1, n_experts):
            give_back(which, c, k).wait_recv()
        return [
            jnp.dot(gather, rows, preferred_element_type=jnp.float32)
            for rows in take_slots(bak.at[which], c)
        ]

    def gradient_piece(c, total):
        for j, d in enumerate(from_slots(DROW, c, gather_b)):
            at = cols(2 * c + j)
            scaled = d * gain_ref[:, at]
            dn[:, at] = scaled
            total = total + jnp.sum(
                scaled * saved_ref[0, :, at].astype(jnp.float32), axis=-1, keepdims=True
            )
        return total

    total = lax.fori_loop(0, chunks, gradient_piece, jnp.zeros((tokens, 1), jnp.float32))
    pull = total * (1.0 / dim) * scale_b * scale_b * scale_b
    dx_ref[0] = (
        gy_buf[...].astype(jnp.float32)
        + (dn[...] * scale_b - saved_ref[0].astype(jnp.float32) * pull)
    ).astype(jnp.bfloat16)

    gates = as_column(fwd_gates_ref[...])

    @pl.loop(0, chunks)
    def _(c):
        for j, e in enumerate(from_slots(EOUT, c, gather_f)):
            at = cols(2 * c + j)
            out_ref[0, :, at] = (x_buf[:, at].astype(jnp.float32) + e * gates).astype(jnp.bfloat16)

    for w in range(2):
        pipe_sent(w)
    for m in range(2):
        for i in range(13):
            weight_copy(m, i).wait_send()

    @pl.loop(0, chunks)
    def _(c):
        for k in range(1, n_experts):
            for which in range(3):
                dispatch(which, c, k).wait_send()
            for which in range(2):
                give_back(which, c, k).wait_send()


def local(
    act_prev,
    fwd_routes,
    fwd_gates,
    saved_input,
    grad_prev,
    bwd_routes,
    bwd_gates,
    norm_gain,
    w_up,
    w_down,
):
    n_pipe = lax.axis_size("pipe")
    n_x, n_y = 4, 4
    n_experts = lax.axis_size("expert") // (2 * n_x)
    tokens, dim = act_prev.shape[1], act_prev.shape[2]
    hidden, width = w_up.shape[2], w_up.shape[3]
    cap = 3 * tokens // (2 * n_experts)
    blocks = dim // width
    chunks = blocks // 2
    slots = n_experts * cap
    bf16, f32 = jnp.bfloat16, jnp.float32
    dma = pltpu.SemaphoreType.DMA
    vmem, hbm = pl.BlockSpec(memory_space=pltpu.VMEM), pl.BlockSpec(memory_space=pltpu.HBM)
    return pl.pallas_call(
        functools.partial(kernel, (n_pipe, n_y, n_experts, n_x, cap, chunks, width)),
        out_shape=[jax.ShapeDtypeStruct(act_prev.shape, bf16)] * 2,
        in_specs=[hbm] * 10,
        out_specs=[vmem, vmem],
        scratch_shapes=[
            pltpu.VMEM((1, tokens), jnp.int32),
            pltpu.VMEM((1, tokens), f32),
            pltpu.VMEM((1, tokens, dim), bf16),
            pltpu.VMEM((1, tokens), jnp.int32),
            pltpu.VMEM((1, tokens), f32),
            pltpu.VMEM((1, dim), f32),
            pltpu.VMEM((tokens, dim), bf16),
            pltpu.VMEM((tokens, dim), bf16),
            pltpu.VMEM((2, tokens // n_y, dim), bf16),
            pltpu.VMEM((blocks, hidden, width), bf16),
            pltpu.VMEM((blocks, hidden, width), bf16),
            pltpu.VMEM((tokens, dim), bf16),
            pltpu.VMEM((3, chunks, n_experts - 1, 2 * cap, width), bf16),
            pltpu.VMEM((3, chunks, n_experts, 2 * cap, width), bf16),
            pltpu.VMEM((2, chunks, n_experts - 1, 2 * cap, width), bf16),
            pltpu.VMEM((2, chunks, n_experts, 2 * cap, width), bf16),
            pltpu.VMEM((slots, hidden), f32),
            pltpu.VMEM((slots, hidden), f32),
            pltpu.VMEM((slots, hidden), bf16),
            pltpu.VMEM((tokens, dim), f32),
            dma((6,)),
            dma((2, n_y)),
            dma((2, n_y)),
            dma((2,)),
            dma((2,)),
            dma((2, 13)),
            dma((2, 13)),
            dma((2,)),
            dma((3, chunks, n_experts - 1)),
            dma((3, chunks, n_experts - 1)),
            dma((2, chunks, n_experts - 1)),
            dma((2, chunks, n_experts - 1)),
        ],
        compiler_params=pltpu.CompilerParams(
            collective_id=0, has_side_effects=True, vmem_limit_bytes=105 * 2**19
        ),
        cost_estimate=pl.CostEstimate(
            flops=10 * slots * hidden * dim, bytes_accessed=24 * 2**20, transcendentals=0
        ),
    )(
        act_prev,
        fwd_routes.reshape(1, tokens),
        fwd_gates.reshape(1, tokens),
        saved_input,
        grad_prev,
        bwd_routes.reshape(1, tokens),
        bwd_gates.reshape(1, tokens),
        norm_gain,
        w_up,
        w_down,
    )


def solution(mesh):
    rows = P("pipe", "expert", None)
    blocks = P("pipe", "expert", None, None)
    return jax.shard_map(
        local,
        mesh=mesh,
        in_specs=(rows,) * 7 + (P("pipe", None), blocks, blocks),
        out_specs=(rows, rows),
        check_vma=False,
    )
```

```python
import functools

import jax
import jax.numpy as jnp
from jax import lax
from jax.experimental import pallas as pl
from jax.experimental.pallas import tpu as pltpu
from jax.sharding import PartitionSpec as P

MESH = pl.DeviceIdType.MESH
EPS = 1e-06
ROWS, COT, FWD = 0, 1, 2
DROW, EOUT = 0, 1
TRANS_RHS = (((1,), (1,)), ((), ()))


def as_column(row):
    n = row.shape[1]
    down = lax.broadcasted_iota(jnp.int32, (n, n), 0)
    across = lax.broadcasted_iota(jnp.int32, (n, n), 1)
    return jnp.sum(jnp.where(down == across, row, 0.0), axis=1, keepdims=True)


def slot_masks(routes, here, n_experts, capacity):
    tokens = routes.shape[1]
    as_row = lax.rem(routes - here + n_experts, n_experts).astype(jnp.float32)
    relative = as_column(as_row)
    down = lax.broadcasted_iota(jnp.int32, (tokens, tokens), 0)
    across = lax.broadcasted_iota(jnp.int32, (tokens, tokens), 1)
    same = jnp.where(relative == as_row, 1.0, 0.0)
    rank_col = jnp.sum(jnp.where(across < down, same, 0.0), axis=1, keepdims=True)
    rank_row = jnp.sum(jnp.where(down < across, same, 0.0), axis=0, keepdims=True)
    slots = n_experts * capacity
    target_col = (relative * capacity + rank_col).astype(jnp.int32)
    target_row = (as_row * capacity + rank_row).astype(jnp.int32)
    slot_of_col = lax.broadcasted_iota(jnp.int32, (tokens, slots), 1)
    slot_of_row = lax.broadcasted_iota(jnp.int32, (slots, tokens), 0)
    gather = jnp.where(target_col == slot_of_col, 1.0, 0.0).astype(jnp.bfloat16)
    pack = jnp.where(target_row == slot_of_row, 1.0, 0.0).astype(jnp.bfloat16)
    return gather, pack


def kernel(
    sizes,
    act_ref,
    fwd_routes_hbm,
    fwd_gates_hbm,
    saved_hbm,
    grad_ref,
    bwd_routes_hbm,
    bwd_gates_hbm,
    gain_hbm,
    up_ref,
    down_ref,
    out_ref,
    dx_ref,
    fwd_routes_ref,
    fwd_gates_ref,
    saved_ref,
    bwd_routes_ref,
    bwd_gates_ref,
    gain_ref,
    x_buf,
    gy_buf,
    passing,
    up_all,
    down_all,
    normed,
    snd,
    rcv,
    ret,
    bak,
    hid,
    dact,
    mid,
    dn,
    load_sem,
    pipe_send,
    pipe_recv,
    relay_send,
    relay_recv,
    w_send,
    w_recv,
    w_own,
    disp_send,
    disp_recv,
    ret_send,
    ret_recv,
):
    n_pipe, n_y, n_experts, n_x, cap, chunks, width = sizes
    tokens = saved_ref.shape[1]
    dim = saved_ref.shape[2]
    per_group = 2 * n_x
    pipe = lax.axis_index("pipe")
    place = lax.axis_index("expert")
    here = place // per_group
    spot = lax.rem(place, per_group)
    my_x, core = spot // 2, lax.rem(spot, 2)

    def spot_of(x, c):
        return lax.rem(x + n_x, n_x) * 2 + c

    def group_peer(offset):
        return (pipe, lax.rem(here + offset + n_experts, n_experts) * per_group + spot)

    right = (pipe, here * per_group + spot_of(my_x + 1, core))
    left = (pipe, here * per_group + spot_of(my_x - 1, core))
    sibling = (pipe, here * per_group + spot_of(my_x, 1 - core))
    later = (lax.rem(pipe + 1, n_pipe), place)
    earlier = (lax.rem(pipe + n_pipe - 1, n_pipe), place)
    my_y, my_z = lax.rem(pipe, n_y), pipe // n_y
    n_z = n_pipe // n_y

    def at_yz(y, z):
        return (lax.rem(z + n_z, n_z) * n_y + y, place)

    barrier = pltpu.get_barrier_semaphore()

    def greet(peer):
        pl.semaphore_signal(barrier, inc=1, device_id=peer, device_id_type=MESH)

    for k in range(1, n_experts):
        greet(group_peer(k))
    for peer in (right, left, sibling):
        greet(peer)
    for k in range(1, n_y):
        greet(at_yz(lax.rem(my_y + k, n_y), my_z))

    @pl.when(my_y == 0)
    def _():
        for y in range(n_y):
            greet(at_yz(y, my_z - 1))

    @pl.when(my_y == n_y - 1)
    def _():
        for y in range(n_y):
            greet(at_yz(y, my_z + 1))

    greetings = (n_experts - 1) + 3 + (n_y - 1) + 2

    loads = [
        pltpu.make_async_copy(src, dst, load_sem.at[i])
        for i, (src, dst) in enumerate(
            (
                (saved_hbm, saved_ref),
                (gain_hbm, gain_ref),
                (bwd_routes_hbm, bwd_routes_ref),
                (bwd_gates_hbm, bwd_gates_ref),
                (fwd_routes_hbm, fwd_routes_ref),
                (fwd_gates_hbm, fwd_gates_ref),
            )
        )
    ]
    for load in loads:
        load.start()

    part = tokens // n_y
    last_y = n_y - 1
    crossing = (my_y == last_y, my_y == 0)
    straight = (last_y, 0)
    relays = (range(0, last_y), range(1, n_y))

    def part_rows(y):
        return pl.ds(y * part, part)

    def remote(src, dst, send_sem, recv_sem, peer):
        return pltpu.make_async_remote_copy(
            src_ref=src,
            dst_ref=dst,
            send_sem=send_sem,
            recv_sem=recv_sem,
            device_id=peer,
            device_id_type=MESH,
        )

    pipe_ends = ((act_ref, x_buf, later), (grad_ref, gy_buf, earlier))

    def pipe_part(w, y):
        src, dst, peer = pipe_ends[w]
        rows = part_rows(y)
        return remote(src.at[0, rows], dst.at[rows], pipe_send.at[w, y], pipe_recv.at[w, y], peer)

    def pipe_to_relay(w, y):
        src = pipe_ends[w][0].at[0, part_rows(y)]
        return remote(src, passing.at[w], pipe_send.at[w, y], relay_recv.at[w], at_yz(y, my_z))

    def pipe_from_relay(w, y):
        peer = (at_yz(0, my_z + 1), at_yz(last_y, my_z - 1))[w]
        dst = pipe_ends[w][1].at[part_rows(y)]
        return remote(passing.at[w], dst, relay_send.at[w], pipe_recv.at[w, y], peer)

    def pipe_start(w):
        @pl.when(crossing[w])
        def _():
            for y in relays[w]:
                pipe_to_relay(w, y).start()
            pipe_part(w, straight[w]).start()

        @pl.when(jnp.logical_not(crossing[w]))
        def _():
            for y in range(n_y):
                pipe_part(w, y).start()

    def pipe_pass_on(w):
        for y in relays[w]:

            @pl.when(my_y == y)
            def _():
                pipe_to_relay(w, y).wait_recv()
                pipe_from_relay(w, y).start()

    def pipe_arrived(w):
        for y in range(n_y):
            pipe_part(w, y).wait_recv()

    def pipe_sent(w):
        for y in range(n_y):
            pipe_part(w, y).wait_send()
        for y in relays[w]:

            @pl.when(my_y == y)
            def _():
                pipe_from_relay(w, y).wait_send()

    def dispatch(which, c, k):
        return pltpu.make_async_remote_copy(
            src_ref=snd.at[which, c, k - 1],
            dst_ref=rcv.at[which, c, k],
            send_sem=disp_send.at[which, c, k - 1],
            recv_sem=disp_recv.at[which, c, k - 1],
            device_id=group_peer(k),
            device_id_type=MESH,
        )

    def give_back(which, c, k):
        return pltpu.make_async_remote_copy(
            src_ref=ret.at[which, c, k - 1],
            dst_ref=bak.at[which, c, k],
            send_sem=ret_send.at[which, c, k - 1],
            recv_sem=ret_recv.at[which, c, k - 1],
            device_id=group_peer(-k),
            device_id_type=MESH,
        )

    half = up_ref.shape[2] // 2
    first, second = pl.ds(0, half), pl.ds(half, half)
    spot_l, spot_r = spot_of(my_x - 1, core), spot_of(my_x + 1, core)
    spot_a = spot_of(my_x + 2, core)
    arrivals = [
        (spot_l, first),
        (spot_l, second),
        (spot_r, first),
        (spot_r, second),
        (spot_a, first),
        (spot_a, second),
    ]

    def weight_copy(m, i):
        own, everything = ((up_ref, up_all), (down_ref, down_all))[m]
        if i < 4:
            rows = (first, second)[i % 2]
            src, dst = own.at[0, 0, rows], everything.at[spot, rows]
            peer = right if i < 2 else left
        elif i == 4:
            src = dst = everything.at[spot_l, first]
            peer = right
        elif i == 5:
            src = dst = everything.at[spot_r, second]
            peer = left
        elif i == 6:
            src, dst, peer = own.at[0, 0], everything.at[spot], sibling
        else:
            at, rows = arrivals[i - 7]
            src = dst = everything.at[at, rows]
            peer = sibling
        return pltpu.make_async_remote_copy(
            src_ref=src,
            dst_ref=dst,
            send_sem=w_send.at[m, i],
            recv_sem=w_recv.at[m, i],
            device_id=peer,
            device_id_type=MESH,
        )

    own_copies = [
        pltpu.make_async_copy(up_ref.at[0, 0], up_all.at[spot], w_own.at[0]),
        pltpu.make_async_copy(down_ref.at[0, 0], down_all.at[spot], w_own.at[1]),
    ]
    for copy in own_copies:
        copy.start()

    def cols(h):
        return pl.ds(pl.multiple_of(h * width, width), width)

    def put_slots(c, low, high, remote, local):
        for k in range(n_experts):
            rows = slice(k * cap, (k + 1) * cap)
            piece = jnp.concatenate([low[rows], high[rows]], axis=0).astype(jnp.bfloat16)
            if k == 0:
                local[c, 0] = piece
            else:
                remote[c, k - 1] = piece

    def take_slots(buf, c):
        whole = [buf[c, k].astype(jnp.float32) for k in range(n_experts)]
        return [
            jnp.concatenate([w[j * cap : (j + 1) * cap] for w in whole], axis=0).astype(jnp.bfloat16)
            for j in range(2)
        ]

    def pack_piece(which, c, pack):
        low, high = [
            jnp.dot(pack, normed[:, cols(2 * c + j)], preferred_element_type=jnp.float32)
            for j in range(2)
        ]
        put_slots(c, low, high, snd.at[which], rcv.at[which])

    def send_piece(which, c):
        for k in range(1, n_experts):
            dispatch(which, c, k).start()

    def scale_of(values):
        return lax.rsqrt(jnp.sum(values * values, axis=-1, keepdims=True) * (1.0 / dim) + EPS)

    for load in loads:
        load.wait()
    gain = gain_ref[...]
    saved = saved_ref[0].astype(jnp.float32)
    scale_b = scale_of(saved)
    normed[...] = (saved * scale_b * gain).astype(jnp.bfloat16)
    gather_b, pack_b = slot_masks(bwd_routes_ref[...], here, n_experts, cap)

    pack_piece(ROWS, 0, pack_b)
    pl.semaphore_wait(barrier, greetings)

    pipe_start(1)
    pipe_start(0)
    send_piece(ROWS, 0)
    for m in range(2):
        for i in (0, 3, 1, 2, 6):
            weight_copy(m, i).start()
    pipe_pass_on(1)

    @pl.loop(1, chunks)
    def _(c):
        pack_piece(ROWS, c, pack_b)
        send_piece(ROWS, c)

    pipe_pass_on(0)


    gates_b = as_column(bwd_gates_ref[...])
    pipe_arrived(1)
    normed[...] = (gy_buf[...].astype(jnp.float32) * gates_b).astype(jnp.bfloat16)

    @pl.loop(0, chunks)
    def _(c):
        pack_piece(COT, c, pack_b)
        send_piece(COT, c)

    gather_f, pack_f = slot_masks(fwd_routes_ref[...], here, n_experts, cap)
    pipe_arrived(0)
    x = x_buf[...].astype(jnp.float32)
    normed[...] = (x * scale_of(x) * gain).astype(jnp.bfloat16)

    @pl.loop(0, chunks)
    def _(c):
        pack_piece(FWD, c, pack_f)
        send_piece(FWD, c)

    def pass_on(m):
        weight_copy(m, 0).wait_recv()
        weight_copy(m, 4).start()
        weight_copy(m, 7).start()
        weight_copy(m, 3).wait_recv()
        weight_copy(m, 5).start()
        weight_copy(m, 10).start()
        for i in (1, 2, 4, 5):
            weight_copy(m, i).wait_recv()
            weight_copy(m, 7 + i).start()

    def have_weights(m):
        own_copies[m].wait()
        for i in range(6, 13):
            weight_copy(m, i).wait_recv()

    def into_hidden(which, weights, total):
        total[...] = jnp.zeros_like(total)

        @pl.loop(0, chunks)
        def _(c):
            for k in range(1, n_experts):
                dispatch(which, c, k).wait_recv()
            for j, rows in enumerate(take_slots(rcv.at[which], c)):
                total[...] += lax.dot_general(
                    rows, weights[2 * c + j], TRANS_RHS, preferred_element_type=jnp.float32
                )

    def out_of_hidden(which, weights):
        @pl.loop(0, chunks)
        def _(c):
            low, high = [
                jnp.dot(mid[...], weights[2 * c + j], preferred_element_type=jnp.float32)
                for j in range(2)
            ]
            put_slots(c, low, high, ret.at[which], bak.at[which])
            for k in range(1, n_experts):
                give_back(which, c, k).start()

    pass_on(0)
    have_weights(0)
    into_hidden(ROWS, up_all, hid)
    pass_on(1)
    have_weights(1)
    into_hidden(COT, down_all, dact)
    h = hid[...]
    sigma = 1.0 / (1.0 + jnp.exp(-h))
    mid[...] = (dact[...] * (sigma * (1.0 + h * (1.0 - sigma)))).astype(jnp.bfloat16)
    out_of_hidden(DROW, up_all)

    into_hidden(FWD, up_all, hid)
    h = hid[...]
    mid[...] = (h / (1.0 + jnp.exp(-h))).astype(jnp.bfloat16)
    out_of_hidden(EOUT, down_all)

    def from_slots(which, c, gather):
        for k in range(1, n_experts):
            give_back(which, c, k).wait_recv()
        return [
            jnp.dot(gather, rows, preferred_element_type=jnp.float32)
            for rows in take_slots(bak.at[which], c)
        ]

    def gradient_piece(c, total):
        for j, d in enumerate(from_slots(DROW, c, gather_b)):
            at = cols(2 * c + j)
            scaled = d * gain_ref[:, at]
            dn[:, at] = scaled
            total = total + jnp.sum(
                scaled * saved_ref[0, :, at].astype(jnp.float32), axis=-1, keepdims=True
            )
        return total

    total = lax.fori_loop(0, chunks, gradient_piece, jnp.zeros((tokens, 1), jnp.float32))
    pull = total * (1.0 / dim) * scale_b * scale_b * scale_b
    dx_ref[0] = (
        gy_buf[...].astype(jnp.float32)
        + (dn[...] * scale_b - saved_ref[0].astype(jnp.float32) * pull)
    ).astype(jnp.bfloat16)

    gates = as_column(fwd_gates_ref[...])

    @pl.loop(0, chunks)
    def _(c):
        for j, e in enumerate(from_slots(EOUT, c, gather_f)):
            at = cols(2 * c + j)
            out_ref[0, :, at] = (x_buf[:, at].astype(jnp.float32) + e * gates).astype(jnp.bfloat16)

    for w in range(2):
        pipe_sent(w)
    for m in range(2):
        for i in range(13):
            weight_copy(m, i).wait_send()

    @pl.loop(0, chunks)
    def _(c):
        for k in range(1, n_experts):
            for which in range(3):
                dispatch(which, c, k).wait_send()
            for which in range(2):
                give_back(which, c, k).wait_send()


def local(
    act_prev,
    fwd_routes,
    fwd_gates,
    saved_input,
    grad_prev,
    bwd_routes,
    bwd_gates,
    norm_gain,
    w_up,
    w_down,
):
    n_pipe = lax.axis_size("pipe")
    n_x, n_y = 4, 4
    n_experts = lax.axis_size("expert") // (2 * n_x)
    tokens, dim = act_prev.shape[1], act_prev.shape[2]
    hidden, width = w_up.shape[2], w_up.shape[3]
    cap = 3 * tokens // (2 * n_experts)
    blocks = dim // width
    chunks = blocks // 2
    slots = n_experts * cap
    bf16, f32 = jnp.bfloat16, jnp.float32
    dma = pltpu.SemaphoreType.DMA
    vmem, hbm = pl.BlockSpec(memory_space=pltpu.VMEM), pl.BlockSpec(memory_space=pltpu.HBM)
    return pl.pallas_call(
        functools.partial(kernel, (n_pipe, n_y, n_experts, n_x, cap, chunks, width)),
        out_shape=[jax.ShapeDtypeStruct(act_prev.shape, bf16)] * 2,
        in_specs=[hbm] * 10,
        out_specs=[vmem, vmem],
        scratch_shapes=[
            pltpu.VMEM((1, tokens), jnp.int32),
            pltpu.VMEM((1, tokens), f32),
            pltpu.VMEM((1, tokens, dim), bf16),
            pltpu.VMEM((1, tokens), jnp.int32),
            pltpu.VMEM((1, tokens), f32),
            pltpu.VMEM((1, dim), f32),
            pltpu.VMEM((tokens, dim), bf16),
            pltpu.VMEM((tokens, dim), bf16),
            pltpu.VMEM((2, tokens // n_y, dim), bf16),
            pltpu.VMEM((blocks, hidden, width), bf16),
            pltpu.VMEM((blocks, hidden, width), bf16),
            pltpu.VMEM((tokens, dim), bf16),
            pltpu.VMEM((3, chunks, n_experts - 1, 2 * cap, width), bf16),
            pltpu.VMEM((3, chunks, n_experts, 2 * cap, width), bf16),
            pltpu.VMEM((2, chunks, n_experts - 1, 2 * cap, width), bf16),
            pltpu.VMEM((2, chunks, n_experts, 2 * cap, width), bf16),
            pltpu.VMEM((slots, hidden), f32),
            pltpu.VMEM((slots, hidden), f32),
            pltpu.VMEM((slots, hidden), bf16),
            pltpu.VMEM((tokens, dim), f32),
            dma((6,)),
            dma((2, n_y)),
            dma((2, n_y)),
            dma((2,)),
            dma((2,)),
            dma((2, 13)),
            dma((2, 13)),
            dma((2,)),
            dma((3, chunks, n_experts - 1)),
            dma((3, chunks, n_experts - 1)),
            dma((2, chunks, n_experts - 1)),
            dma((2, chunks, n_experts - 1)),
        ],
        compiler_params=pltpu.CompilerParams(
            collective_id=0, has_side_effects=True, vmem_limit_bytes=48 * 2**20
        ),
        cost_estimate=pl.CostEstimate(
            flops=10 * slots * hidden * dim, bytes_accessed=24 * 2**20, transcendentals=0
        ),
    )(
        *(
            pltpu.with_memory_space_constraint(operand, pltpu.HBM)
            for operand in (
                act_prev,
                fwd_routes.reshape(1, tokens),
                fwd_gates.reshape(1, tokens),
                saved_input,
                grad_prev,
                bwd_routes.reshape(1, tokens),
                bwd_gates.reshape(1, tokens),
                norm_gain,
                w_up,
                w_down,
            )
        )
    )


def solution(mesh):
    rows = P("pipe", "expert", None)
    blocks = P("pipe", "expert", None, None)
    return jax.shard_map(
        local,
        mesh=mesh,
        in_specs=(rows,) * 7 + (P("pipe", None), blocks, blocks),
        out_specs=(rows, rows),
        check_vma=False,
    )
```

```python
import functools

import jax
import jax.numpy as jnp
from jax import lax
from jax.experimental import pallas as pl
from jax.experimental.pallas import tpu as pltpu
from jax.sharding import PartitionSpec as P

MESH = pl.DeviceIdType.MESH
EPS = 1e-06
ROWS, COT, FWD = 0, 1, 2
DROW, EOUT = 0, 1
TRANS_RHS = (((1,), (1,)), ((), ()))


def as_column(row):
    n = row.shape[1]
    down = lax.broadcasted_iota(jnp.int32, (n, n), 0)
    across = lax.broadcasted_iota(jnp.int32, (n, n), 1)
    return jnp.sum(jnp.where(down == across, row, 0.0), axis=1, keepdims=True)


def slot_masks(routes, here, n_experts, capacity):
    tokens = routes.shape[1]
    as_row = lax.rem(routes - here + n_experts, n_experts).astype(jnp.float32)
    relative = as_column(as_row)
    down = lax.broadcasted_iota(jnp.int32, (tokens, tokens), 0)
    across = lax.broadcasted_iota(jnp.int32, (tokens, tokens), 1)
    same = jnp.where(relative == as_row, 1.0, 0.0)
    rank_col = jnp.sum(jnp.where(across < down, same, 0.0), axis=1, keepdims=True)
    rank_row = jnp.sum(jnp.where(down < across, same, 0.0), axis=0, keepdims=True)
    slots = n_experts * capacity
    target_col = (relative * capacity + rank_col).astype(jnp.int32)
    target_row = (as_row * capacity + rank_row).astype(jnp.int32)
    slot_of_col = lax.broadcasted_iota(jnp.int32, (tokens, slots), 1)
    slot_of_row = lax.broadcasted_iota(jnp.int32, (slots, tokens), 0)
    gather = jnp.where(target_col == slot_of_col, 1.0, 0.0).astype(jnp.bfloat16)
    pack = jnp.where(target_row == slot_of_row, 1.0, 0.0).astype(jnp.bfloat16)
    return gather, pack


def kernel(
    sizes,
    act_ref,
    fwd_routes_hbm,
    fwd_gates_hbm,
    saved_hbm,
    grad_ref,
    bwd_routes_hbm,
    bwd_gates_hbm,
    gain_hbm,
    up_ref,
    down_ref,
    out_ref,
    dx_ref,
    fwd_routes_ref,
    fwd_gates_ref,
    saved_ref,
    bwd_routes_ref,
    bwd_gates_ref,
    gain_ref,
    x_buf,
    gy_buf,
    passing,
    up_all,
    down_all,
    normed,
    snd,
    rcv,
    ret,
    bak,
    hid,
    dact,
    mid,
    dn,
    load_sem,
    pipe_send,
    pipe_recv,
    relay_send,
    relay_recv,
    w_send,
    w_recv,
    w_own,
    disp_send,
    disp_recv,
    ret_send,
    ret_recv,
):
    n_pipe, n_y, n_experts, n_x, cap, chunks, width = sizes
    tokens = saved_ref.shape[1]
    dim = saved_ref.shape[2]
    per_group = 2 * n_x
    pipe = lax.axis_index("pipe")
    place = lax.axis_index("expert")
    here = place // per_group
    spot = lax.rem(place, per_group)
    my_x, core = spot // 2, lax.rem(spot, 2)

    def spot_of(x, c):
        return lax.rem(x + n_x, n_x) * 2 + c

    def group_peer(offset):
        return (pipe, lax.rem(here + offset + n_experts, n_experts) * per_group + spot)

    right = (pipe, here * per_group + spot_of(my_x + 1, core))
    left = (pipe, here * per_group + spot_of(my_x - 1, core))
    sibling = (pipe, here * per_group + spot_of(my_x, 1 - core))
    later = (lax.rem(pipe + 1, n_pipe), place)
    earlier = (lax.rem(pipe + n_pipe - 1, n_pipe), place)
    my_y, my_z = lax.rem(pipe, n_y), pipe // n_y
    n_z = n_pipe // n_y

    def at_yz(y, z):
        return (lax.rem(z + n_z, n_z) * n_y + y, place)

    barrier = pltpu.get_barrier_semaphore()

    def greet(peer):
        pl.semaphore_signal(barrier, inc=1, device_id=peer, device_id_type=MESH)

    for k in range(1, n_experts):
        greet(group_peer(k))
    for peer in (right, left, sibling):
        greet(peer)
    for k in range(1, n_y):
        greet(at_yz(lax.rem(my_y + k, n_y), my_z))

    @pl.when(my_y == 0)
    def _():
        for y in range(n_y):
            greet(at_yz(y, my_z - 1))

    @pl.when(my_y == n_y - 1)
    def _():
        for y in range(n_y):
            greet(at_yz(y, my_z + 1))

    greetings = (n_experts - 1) + 3 + (n_y - 1) + 2

    loads = [
        pltpu.make_async_copy(src, dst, load_sem.at[i])
        for i, (src, dst) in enumerate(
            (
                (saved_hbm, saved_ref),
                (gain_hbm, gain_ref),
                (bwd_routes_hbm, bwd_routes_ref),
                (bwd_gates_hbm, bwd_gates_ref),
                (fwd_routes_hbm, fwd_routes_ref),
                (fwd_gates_hbm, fwd_gates_ref),
            )
        )
    ]
    for load in loads:
        load.start()

    part = tokens // n_y
    last_y = n_y - 1
    crossing = (my_y == last_y, my_y == 0)
    straight = (last_y, 0)
    relays = (range(0, last_y), range(1, n_y))

    def part_rows(y):
        return pl.ds(y * part, part)

    def remote(src, dst, send_sem, recv_sem, peer):
        return pltpu.make_async_remote_copy(
            src_ref=src,
            dst_ref=dst,
            send_sem=send_sem,
            recv_sem=recv_sem,
            device_id=peer,
            device_id_type=MESH,
        )

    pipe_ends = ((act_ref, x_buf, later), (grad_ref, gy_buf, earlier))

    def pipe_part(w, y):
        src, dst, peer = pipe_ends[w]
        rows = part_rows(y)
        return remote(src.at[0, rows], dst.at[rows], pipe_send.at[w, y], pipe_recv.at[w, y], peer)

    def pipe_to_relay(w, y):
        src = pipe_ends[w][0].at[0, part_rows(y)]
        return remote(src, passing.at[w], pipe_send.at[w, y], relay_recv.at[w], at_yz(y, my_z))

    def pipe_from_relay(w, y):
        peer = (at_yz(0, my_z + 1), at_yz(last_y, my_z - 1))[w]
        dst = pipe_ends[w][1].at[part_rows(y)]
        return remote(passing.at[w], dst, relay_send.at[w], pipe_recv.at[w, y], peer)

    def pipe_start(w):
        @pl.when(crossing[w])
        def _():
            for y in relays[w]:
                pipe_to_relay(w, y).start()
            pipe_part(w, straight[w]).start()

        @pl.when(jnp.logical_not(crossing[w]))
        def _():
            for y in range(n_y):
                pipe_part(w, y).start()

    def pipe_pass_on(w):
        for y in relays[w]:

            @pl.when(my_y == y)
            def _():
                pipe_to_relay(w, y).wait_recv()
                pipe_from_relay(w, y).start()

    def pipe_arrived(w):
        for y in range(n_y):
            pipe_part(w, y).wait_recv()

    def pipe_sent(w):
        for y in range(n_y):
            pipe_part(w, y).wait_send()
        for y in relays[w]:

            @pl.when(my_y == y)
            def _():
                pipe_from_relay(w, y).wait_send()

    def dispatch(which, c, k):
        return pltpu.make_async_remote_copy(
            src_ref=snd.at[which, c, k - 1],
            dst_ref=rcv.at[which, c, k],
            send_sem=disp_send.at[which, c, k - 1],
            recv_sem=disp_recv.at[which, c, k - 1],
            device_id=group_peer(k),
            device_id_type=MESH,
        )

    def give_back(which, c, k):
        return pltpu.make_async_remote_copy(
            src_ref=ret.at[which, c, k - 1],
            dst_ref=bak.at[which, c, k],
            send_sem=ret_send.at[which, c, k - 1],
            recv_sem=ret_recv.at[which, c, k - 1],
            device_id=group_peer(-k),
            device_id_type=MESH,
        )

    half = up_ref.shape[2] // 2
    first, second = pl.ds(0, half), pl.ds(half, half)
    spot_l, spot_r = spot_of(my_x - 1, core), spot_of(my_x + 1, core)
    spot_a = spot_of(my_x + 2, core)
    arrivals = [
        (spot_l, first),
        (spot_l, second),
        (spot_r, first),
        (spot_r, second),
        (spot_a, first),
        (spot_a, second),
    ]

    def weight_copy(m, i):
        own, everything = ((up_ref, up_all), (down_ref, down_all))[m]
        if i < 4:
            rows = (first, second)[i % 2]
            src, dst = own.at[0, 0, rows], everything.at[spot, rows]
            peer = right if i < 2 else left
        elif i == 4:
            src = dst = everything.at[spot_l, first]
            peer = right
        elif i == 5:
            src = dst = everything.at[spot_r, second]
            peer = left
        elif i == 6:
            src, dst, peer = own.at[0, 0], everything.at[spot], sibling
        else:
            at, rows = arrivals[i - 7]
            src = dst = everything.at[at, rows]
            peer = sibling
        return pltpu.make_async_remote_copy(
            src_ref=src,
            dst_ref=dst,
            send_sem=w_send.at[m, i],
            recv_sem=w_recv.at[m, i],
            device_id=peer,
            device_id_type=MESH,
        )

    own_copies = [
        pltpu.make_async_copy(up_ref.at[0, 0], up_all.at[spot], w_own.at[0]),
        pltpu.make_async_copy(down_ref.at[0, 0], down_all.at[spot], w_own.at[1]),
    ]
    for copy in own_copies:
        copy.start()

    def cols(h):
        return pl.ds(pl.multiple_of(h * width, width), width)

    def put_slots(c, low, high, remote, local):
        for k in range(n_experts):
            rows = slice(k * cap, (k + 1) * cap)
            piece = jnp.concatenate([low[rows], high[rows]], axis=0).astype(jnp.bfloat16)
            if k == 0:
                local[c, 0] = piece
            else:
                remote[c, k - 1] = piece

    def take_slots(buf, c):
        whole = [buf[c, k].astype(jnp.float32) for k in range(n_experts)]
        return [
            jnp.concatenate([w[j * cap : (j + 1) * cap] for w in whole], axis=0).astype(jnp.bfloat16)
            for j in range(2)
        ]

    def pack_piece(which, c, pack):
        low, high = [
            jnp.dot(pack, normed[:, cols(2 * c + j)], preferred_element_type=jnp.float32)
            for j in range(2)
        ]
        put_slots(c, low, high, snd.at[which], rcv.at[which])

    def send_piece(which, c):
        for k in range(1, n_experts):
            dispatch(which, c, k).start()

    def scale_of(values):
        return lax.rsqrt(jnp.sum(values * values, axis=-1, keepdims=True) * (1.0 / dim) + EPS)

    for load in loads:
        load.wait()
    gain = gain_ref[...]
    saved = saved_ref[0].astype(jnp.float32)
    scale_b = scale_of(saved)
    normed[...] = (saved * scale_b * gain).astype(jnp.bfloat16)
    gather_b, pack_b = slot_masks(bwd_routes_ref[...], here, n_experts, cap)

    pack_piece(ROWS, 0, pack_b)
    pl.semaphore_wait(barrier, greetings)

    pipe_start(1)
    pipe_start(0)
    send_piece(ROWS, 0)
    for m in range(2):
        for i in (0, 3, 1, 2, 6):
            weight_copy(m, i).start()
    pipe_pass_on(1)

    @pl.loop(1, chunks)
    def _(c):
        pack_piece(ROWS, c, pack_b)
        send_piece(ROWS, c)

    pipe_pass_on(0)


    gates_b = as_column(bwd_gates_ref[...])
    pipe_arrived(1)
    normed[...] = (gy_buf[...].astype(jnp.float32) * gates_b).astype(jnp.bfloat16)

    @pl.loop(0, chunks)
    def _(c):
        pack_piece(COT, c, pack_b)
        send_piece(COT, c)

    gather_f, pack_f = slot_masks(fwd_routes_ref[...], here, n_experts, cap)
    pipe_arrived(0)
    x = x_buf[...].astype(jnp.float32)
    normed[...] = (x * scale_of(x) * gain).astype(jnp.bfloat16)

    @pl.loop(0, chunks)
    def _(c):
        pack_piece(FWD, c, pack_f)
        send_piece(FWD, c)

    def pass_on(m):
        weight_copy(m, 0).wait_recv()
        weight_copy(m, 4).start()
        weight_copy(m, 7).start()
        weight_copy(m, 3).wait_recv()
        weight_copy(m, 5).start()
        weight_copy(m, 10).start()
        for i in (1, 2, 4, 5):
            weight_copy(m, i).wait_recv()
            weight_copy(m, 7 + i).start()

    def have_weights(m):
        own_copies[m].wait()
        for i in range(6, 13):
            weight_copy(m, i).wait_recv()

    def into_hidden(which, weights, total):
        total[...] = jnp.zeros_like(total)

        @pl.loop(0, chunks)
        def _(c):
            for k in range(1, n_experts):
                dispatch(which, c, k).wait_recv()
            for j, rows in enumerate(take_slots(rcv.at[which], c)):
                total[...] += lax.dot_general(
                    rows, weights[2 * c + j], TRANS_RHS, preferred_element_type=jnp.float32
                )

    def out_of_hidden(which, weights):
        @pl.loop(0, chunks)
        def _(c):
            low, high = [
                jnp.dot(mid[...], weights[2 * c + j], preferred_element_type=jnp.float32)
                for j in range(2)
            ]
            put_slots(c, low, high, ret.at[which], bak.at[which])
            for k in range(1, n_experts):
                give_back(which, c, k).start()

    pass_on(0)
    have_weights(0)
    into_hidden(ROWS, up_all, hid)
    pass_on(1)
    have_weights(1)
    into_hidden(COT, down_all, dact)
    h = hid[...]
    sigma = 1.0 / (1.0 + jnp.exp(-h))
    mid[...] = (dact[...] * (sigma * (1.0 + h * (1.0 - sigma)))).astype(jnp.bfloat16)
    out_of_hidden(DROW, up_all)

    into_hidden(FWD, up_all, hid)
    h = hid[...]
    mid[...] = (h / (1.0 + jnp.exp(-h))).astype(jnp.bfloat16)
    out_of_hidden(EOUT, down_all)

    def from_slots(which, c, gather):
        for k in range(1, n_experts):
            give_back(which, c, k).wait_recv()
        return [
            jnp.dot(gather, rows, preferred_element_type=jnp.float32)
            for rows in take_slots(bak.at[which], c)
        ]

    def gradient_piece(c, total):
        for j, d in enumerate(from_slots(DROW, c, gather_b)):
            at = cols(2 * c + j)
            scaled = d * gain_ref[:, at]
            dn[:, at] = scaled
            total = total + jnp.sum(
                scaled * saved_ref[0, :, at].astype(jnp.float32), axis=-1, keepdims=True
            )
        return total

    total = lax.fori_loop(0, chunks, gradient_piece, jnp.zeros((tokens, 1), jnp.float32))
    pull = total * (1.0 / dim) * scale_b * scale_b * scale_b
    dx_ref[0] = (
        gy_buf[...].astype(jnp.float32)
        + (dn[...] * scale_b - saved_ref[0].astype(jnp.float32) * pull)
    ).astype(jnp.bfloat16)

    for w in range(2):
        pipe_sent(w)
    for m in range(2):
        for i in range(13):
            weight_copy(m, i).wait_send()

    @pl.loop(0, chunks)
    def _(c):
        for k in range(1, n_experts):
            for which in range(3):
                dispatch(which, c, k).wait_send()
            give_back(DROW, c, k).wait_send()

    gates = as_column(fwd_gates_ref[...])

    @pl.loop(0, chunks)
    def _(c):
        for j, e in enumerate(from_slots(EOUT, c, gather_f)):
            at = cols(2 * c + j)
            out_ref[0, :, at] = (x_buf[:, at].astype(jnp.float32) + e * gates).astype(jnp.bfloat16)

    @pl.loop(0, chunks)
    def _(c):
        for k in range(1, n_experts):
            give_back(EOUT, c, k).wait_send()


def local(
    act_prev,
    fwd_routes,
    fwd_gates,
    saved_input,
    grad_prev,
    bwd_routes,
    bwd_gates,
    norm_gain,
    w_up,
    w_down,
):
    n_pipe = lax.axis_size("pipe")
    n_x, n_y = 4, 4
    n_experts = lax.axis_size("expert") // (2 * n_x)
    tokens, dim = act_prev.shape[1], act_prev.shape[2]
    hidden, width = w_up.shape[2], w_up.shape[3]
    cap = 3 * tokens // (2 * n_experts)
    blocks = dim // width
    chunks = blocks // 2
    slots = n_experts * cap
    bf16, f32 = jnp.bfloat16, jnp.float32
    dma = pltpu.SemaphoreType.DMA
    vmem, hbm = pl.BlockSpec(memory_space=pltpu.VMEM), pl.BlockSpec(memory_space=pltpu.HBM)
    return pl.pallas_call(
        functools.partial(kernel, (n_pipe, n_y, n_experts, n_x, cap, chunks, width)),
        out_shape=[jax.ShapeDtypeStruct(act_prev.shape, bf16)] * 2,
        in_specs=[hbm] * 10,
        out_specs=[vmem, vmem],
        scratch_shapes=[
            pltpu.VMEM((1, tokens), jnp.int32),
            pltpu.VMEM((1, tokens), f32),
            pltpu.VMEM((1, tokens, dim), bf16),
            pltpu.VMEM((1, tokens), jnp.int32),
            pltpu.VMEM((1, tokens), f32),
            pltpu.VMEM((1, dim), f32),
            pltpu.VMEM((tokens, dim), bf16),
            pltpu.VMEM((tokens, dim), bf16),
            pltpu.VMEM((2, tokens // n_y, dim), bf16),
            pltpu.VMEM((blocks, hidden, width), bf16),
            pltpu.VMEM((blocks, hidden, width), bf16),
            pltpu.VMEM((tokens, dim), bf16),
            pltpu.VMEM((3, chunks, n_experts - 1, 2 * cap, width), bf16),
            pltpu.VMEM((3, chunks, n_experts, 2 * cap, width), bf16),
            pltpu.VMEM((2, chunks, n_experts - 1, 2 * cap, width), bf16),
            pltpu.VMEM((2, chunks, n_experts, 2 * cap, width), bf16),
            pltpu.VMEM((slots, hidden), f32),
            pltpu.VMEM((slots, hidden), f32),
            pltpu.VMEM((slots, hidden), bf16),
            pltpu.VMEM((tokens, dim), f32),
            dma((6,)),
            dma((2, n_y)),
            dma((2, n_y)),
            dma((2,)),
            dma((2,)),
            dma((2, 13)),
            dma((2, 13)),
            dma((2,)),
            dma((3, chunks, n_experts - 1)),
            dma((3, chunks, n_experts - 1)),
            dma((2, chunks, n_experts - 1)),
            dma((2, chunks, n_experts - 1)),
        ],
        compiler_params=pltpu.CompilerParams(
            collective_id=0, has_side_effects=True, vmem_limit_bytes=48 * 2**20
        ),
        cost_estimate=pl.CostEstimate(
            flops=10 * slots * hidden * dim, bytes_accessed=24 * 2**20, transcendentals=0
        ),
    )(
        *(
            pltpu.with_memory_space_constraint(operand, pltpu.HBM)
            for operand in (
                act_prev,
                fwd_routes.reshape(1, tokens),
                fwd_gates.reshape(1, tokens),
                saved_input,
                grad_prev,
                bwd_routes.reshape(1, tokens),
                bwd_gates.reshape(1, tokens),
                norm_gain,
                w_up,
                w_down,
            )
        )
    )


def solution(mesh):
    rows = P("pipe", "expert", None)
    blocks = P("pipe", "expert", None, None)
    return jax.shard_map(
        local,
        mesh=mesh,
        in_specs=(rows,) * 7 + (P("pipe", None), blocks, blocks),
        out_specs=(rows, rows),
        check_vma=False,
    )
```
